128 devices in a mesh: row: 16 (over y_lo, x, core), col: 8 (over y_hi, z).
Axes of the slice: x: 4, y: 4 (y_hi: 2, y_lo: 2; y = y_hi * 2 + y_lo), z: 4, core: 2. Of those that a mesh axis runs over, the one named last changes fastest.
Arguments:
- resid: bfloat16 [2048, 5120], P('row', 'col'), may hold values from -160 to 160
- queries: bfloat16 [2048, 5120], P('row', 'col'), may hold values from -24 to 24
- keys: bfloat16 [2048, 5120], P('row', 'col'), may hold values from -24 to 24
- values: bfloat16 [2048, 5120], P('row', 'col'), may hold values from -6 to 6
- doc_ids: int32 [2048], replicated, may hold values from 0 to 7, never falling along the last dimension, each value on 1 to 1536 neighbouring positions
- norm_gain: float32 [5120], replicated, may hold values from 0.1 to 1.9
- expert_ids: int32 [2048, 6], P('row'), may hold values from 0 to 31, all different within a row; in each aligned block of 128 rows (0 to 127, 128 to 255, ...) at most 32 rows name the same one
- gate_levels: int32 [2048, 6], P('row'), may hold values from 1 to 64
- w_gate: bfloat16 [32, 1536, 5120], P('row', 'col'), may hold values from -0.078125 to 0.078125
- w_up: bfloat16 [32, 1536, 5120], P('row', 'col'), may hold values from -0.078125 to 0.078125
- w_down: bfloat16 [32, 1536, 5120], P('row', 'col'), may hold values from -0.15625 to 0.15625
- cotangent: bfloat16 [2048, 5120], P('row', 'col'), may hold values from -6 to 6
Outputs:
- d_normed: bfloat16 [2048, 5120], P('row', 'col')
- d_w_gate: bfloat16 [32, 1536, 5120], P('row', 'col')
- d_w_up: bfloat16 [32, 1536, 5120], P('row', 'col')
- d_w_down: bfloat16 [32, 1536, 5120], P('row', 'col')
The draws below stay inside these ranges and needn't reach their ends.
Inputs may be any that keep to these rules, and one draw needn't show every extreme that they name: `doc_ids`: document numbers never fall along the tokens; one document spans exactly 1536 tokens. `expert_ids`: each token names 6 different experts. In each aligned block of 128 tokens (the tokens of one row index) no expert is named by more than 32 tokens, a bound that some block reaches.
All inputs are finite; a program needn't handle non-finite values.
Results may differ from the reference program's by a relative error of at most 0.017.
Values may be sent and summed in bfloat16 or wider, within the bound.
No kernel may reach another device: no remote copies, remote signals or barrier semaphores. Data moves between devices by JAX's collectives and lax.ppermute only.
A program may use at most 256 MiB of HBM per device.

```python
import math
import jax
import jax.numpy as jnp
import numpy as np
from jax import lax

D = 5120
HEADS = 40
HEAD_DIM = 128
FF = 1536
TOP = 6
WINDOW = 1024
TOK_ROW = 128
TOKENS = 2048
EXPERTS = 32
CAP = 32
FBLOCK = 192
DOCS = 8
N_ROW = 16
N_COL = 8


def draw_queries(key, part):
    key = jax.random.fold_in(key, 5)
    return jnp.clip(jax.random.normal(key, (TOKENS, D), jnp.float32), -4.0, 4.0).astype(jnp.bfloat16)


def draw_keys(key, part):
    key = jax.random.fold_in(key, 9)
    return jnp.clip(jax.random.normal(key, (TOKENS, D), jnp.float32), -4.0, 4.0).astype(jnp.bfloat16)


def draw_values(key, part):
    key = jax.random.fold_in(key, 7)
    noise_key, phase_key = jax.random.split(key)
    phases = jax.random.uniform(phase_key, (1, D), jnp.float32, 0.0, 2.0 * math.pi)
    positions = jnp.arange(TOKENS, dtype=jnp.int32).astype(jnp.float32)[:, None]
    noise = jnp.clip(jax.random.normal(noise_key, (TOKENS, D), jnp.float32), -4.0, 4.0)
    amplitude = 2.0
    return (noise + amplitude * jnp.sin(math.pi * positions / WINDOW + phases)).astype(jnp.bfloat16)


def draw_resid(key, part):
    key = jax.random.fold_in(key, 3)
    value_key, row_key, col_key = jax.random.split(key, 3)
    normal_part = jnp.clip(jax.random.normal(value_key, (TOKENS, D), jnp.float32), -5.0, 5.0)
    row_scale = jnp.exp(jax.random.uniform(row_key, (TOKENS, 1), jnp.float32, 0.0, math.log(10.0)))
    col_scale = jnp.exp(jax.random.uniform(col_key, (1, D), jnp.float32, 0.0, math.log(10.0)))
    return (0.3 * normal_part * row_scale * col_scale).astype(jnp.bfloat16)


def with_ends(array, stream_key, smallest, largest):
    extent = array.shape
    spot = [jax.random.randint(jax.random.fold_in(stream_key, axis), (), 0, extent[axis]) for axis in range(len(extent))]
    array = array.at[tuple(spot)].set(smallest)
    longest = extent.index(max(extent))
    spot[longest] = (spot[longest] + 1) % extent[longest]
    return array.at[tuple(spot)].set(largest)


def block_levels(key, dims, pieces, low, high):
    def one(dim, parts):
        heights = jax.random.uniform(jax.random.fold_in(jax.random.fold_in(key, 6), dim), (parts,), jnp.float32, low / len(pieces), high / len(pieces))
        return jnp.repeat(jnp.exp(heights), dims[dim] // parts).reshape((-1,) + (1,) * (len(dims) - dim - 1))

    loudness = one(*pieces[0])
    for cut in pieces[1:]:
        loudness = loudness * one(*cut)
    return loudness


def length_profile(amount, total, most, slope):
    loads = [(1 << 20) // math.isqrt(standing ** slope) + 1 for standing in range(2, amount + 1)]
    rest, given = total - most - (amount - 1), [1] * (amount - 1)
    while rest > 0:
        candidates = [i for i in range(amount - 1) if given[i] < most]
        whole, remaining = sum([loads[i] for i in candidates]), rest
        for i in candidates:
            more = min(most - given[i], max(1, remaining * loads[i] // whole), rest)
            given[i] = given[i] + more
            rest = rest - more
    return np.array([most] + given)


def ragged(rng, count, total, most, slope):
    if count == 2:
        one = jax.random.randint(rng, (), max(1, total - most), min(most, total - 1) + 1)
        return jnp.stack([one, total - one])
    sizes = jnp.asarray(length_profile(count, total, most, slope), jnp.int32)
    twos = (count - 1) // 2
    giver, receiver = sizes[1:1 + 2 * twos:2], sizes[2:2 + 2 * twos:2]
    margin = jnp.minimum(giver - 1, most - receiver)
    moved = jax.random.randint(jax.random.fold_in(rng, 1), (twos,), 0, 1 << 20) % (margin + 1)
    sizes = sizes.at[1:1 + 2 * twos:2].set(giver - moved).at[2:2 + 2 * twos:2].set(receiver + moved)
    return sizes[jax.random.permutation(jax.random.fold_in(rng, 2), count)]


def assign_block(key, own, number, rows, amount, top, limit, lean):
    ranking = jax.random.permutation(key, amount)
    packed, usual = portions_of(amount, rows * top, limit, lean, True), portions_of(amount, rows * top, limit, lean, False)
    places = jnp.arange(amount)

    def named(sizes, turn):
        used = int((sizes > 0).sum())
        fixed = max(1, used // 4)
        passed = fixed + (places - fixed + turn * (used - fixed)) % max(1, amount - fixed)
        return jnp.zeros((amount,), jnp.int32).at[ranking[jnp.where(places < fixed, places, passed)]].set(jnp.asarray(sizes, jnp.int32))

    sizes = jnp.where(number % 4 == 0, named(packed, number // 4), named(usual, number - number // 4 - 1))
    mixed = jax.random.permutation(jax.random.fold_in(own, 3), amount)
    source_of, taker = mixed[0:amount // 2 * 2:2], mixed[1:amount // 2 * 2:2]
    slack = jnp.minimum(sizes[source_of] - 1, limit - sizes[taker]) // 2
    slack = jnp.where((source_of == ranking[0]) | (taker == ranking[0]) | (sizes[taker] == 0), 0, jnp.maximum(slack, 0))
    passed = jax.random.randint(jax.random.fold_in(own, 4), (amount // 2,), 0, 1 << 20) % (slack + 1)
    sizes = sizes.at[source_of].add(-passed).at[taker].add(passed)
    items = jnp.searchsorted(jnp.cumsum(sizes), jnp.arange(rows * top), side="right").astype(jnp.int32)
    table = items.reshape(top, rows).T
    table = table[jax.random.permutation(jax.random.fold_in(own, 1), rows)]
    turn = jax.random.randint(jax.random.fold_in(own, 2), (rows, 1), 0, top)
    return jnp.take_along_axis(table, (jnp.arange(top)[None, :] + turn) % top, axis=1)


def portions_of(count, total, limit, lean, full):
    weights = [(1 << 20) // math.isqrt(rank ** lean) + 1 for rank in range(1, count + 1)]
    largest = limit if full else min(limit, max(-(-total // count), total * weights[0] // sum(weights)))
    least = 1 if total - largest >= count - 1 else 0
    given, surplus = [largest] + [least] * (count - 1), total - largest - least * (count - 1)
    while surplus > 0:
        candidates = [i for i in range(1, count) if given[i] < largest] or [i for i in range(1, count) if given[i] < limit]
        mass, remaining = sum([weights[i] for i in candidates]), surplus
        for i in candidates:
            extra = min(limit - given[i], max(1, remaining * weights[i] // mass), surplus)
            given[i] = given[i] + extra
            surplus = surplus - extra
    return np.array(given)


def scatter_about(key, shape, scale, limit, cuts=(), kind=jnp.bfloat16):
    entries = jax.random.normal(key, shape, jnp.float32) * scale
    if len(cuts) > 0:
        entries = block_levels(key, shape, cuts, -0.22, 0.18) * entries
    return jnp.clip(entries, min=-limit, max=limit).astype(kind)


def setup_inputs(seed: int = 0) -> dict:
    arg_keys = jax.random.split(jax.random.key(seed), 13)
    resid = draw_resid(jax.random.fold_in(arg_keys[12], 71), 0)
    queries = draw_queries(jax.random.fold_in(arg_keys[12], 71), 0)
    keys = draw_keys(jax.random.fold_in(arg_keys[12], 71), 0)
    values = draw_values(jax.random.fold_in(arg_keys[12], 71), 0)
    doc_ids = jnp.searchsorted(jnp.cumsum(ragged(arg_keys[4], DOCS, TOKENS, 3 * TOKENS // 4, 2)), jnp.arange(TOKENS), side="right").astype(jnp.int32)
    norm_gain = jnp.clip(1.0 + 0.18 * jax.random.normal(arg_keys[5], (D,), jnp.float32), 0.1, 1.9)
    expert_ids_keys = jax.random.split(jax.random.fold_in(arg_keys[6], 1), TOKENS // TOK_ROW)
    expert_ids_turns = jax.random.permutation(jax.random.fold_in(arg_keys[6], 3), TOKENS // TOK_ROW)
    expert_ids = jax.vmap(lambda own, number: assign_block(jax.random.fold_in(arg_keys[6], 2), own, number, TOK_ROW, EXPERTS, TOP, CAP, 2))(expert_ids_keys, expert_ids_turns).reshape((TOKENS, TOP))
    gate_levels = with_ends(jax.random.randint(arg_keys[7], (TOKENS, TOP), 1, 65), jax.random.fold_in(arg_keys[7], 1), 1, 64).astype(jnp.int32)
    w_gate = scatter_about(arg_keys[8], (EXPERTS, FF, D), D ** -0.5, 0.078125, ((0, 16), (1, 8)))
    w_up = scatter_about(arg_keys[9], (EXPERTS, FF, D), D ** -0.5, 0.078125, ((0, 16), (1, 8)))
    w_down = scatter_about(arg_keys[10], (EXPERTS, FF, D), FF ** -0.5, 0.15625, ((0, 16), (1, 8)))
    cotangent = scatter_about(arg_keys[11], (TOKENS, D), 1.0, 6.0, ((0, 16), (1, 8)))
    return {"resid": resid, "queries": queries, "keys": keys, "values": values, "doc_ids": doc_ids, "norm_gain": norm_gain, "expert_ids": expert_ids, "gate_levels": gate_levels, "w_gate": w_gate, "w_up": w_up, "w_down": w_down, "cotangent": cotangent}


def reference(resid, queries, keys, values, doc_ids, norm_gain, expert_ids, gate_levels, w_gate, w_up, w_down, cotangent):
    positions = jnp.arange(TOKENS, dtype=jnp.int32)
    pos_delta = positions[:, None] - positions[None, :]
    allowed = (pos_delta >= 0) & (pos_delta < WINDOW) & (doc_ids[:, None] == doc_ids[None, :])

    def by_head(matrix):
        return matrix.reshape(TOKENS, HEADS, HEAD_DIM).transpose(1, 0, 2)

    def one_head(operands):
        query_h, key_h, value_h = operands
        scores = jnp.dot(query_h, key_h.T, preferred_element_type=jnp.float32) * (1.0 / math.sqrt(HEAD_DIM))
        scores = jnp.where(allowed, scores, -1e+30)
        top_score = lax.optimization_barrier(jnp.max(scores, axis=1, keepdims=True))
        weights = jnp.exp(scores - top_score)
        probs = (weights / lax.optimization_barrier(jnp.sum(weights, axis=1, keepdims=True))).astype(jnp.bfloat16)
        return jnp.dot(probs, value_h, preferred_element_type=jnp.float32)
    head_out = lax.map(one_head, (by_head(queries), by_head(keys), by_head(values)))
    attention = head_out.transpose(1, 0, 2).reshape(TOKENS, D)
    hidden_in = (resid.astype(jnp.float32) + attention).astype(jnp.bfloat16)
    widened = hidden_in.astype(jnp.float32)
    inv_rms = lax.rsqrt(lax.optimization_barrier(jnp.mean(widened * widened, axis=1, keepdims=True)) + 1e-05)
    normed = (widened * inv_rms * norm_gain[None, :]).astype(jnp.bfloat16)
    block_ids = expert_ids.reshape(N_ROW, TOK_ROW * TOP)
    matches = (block_ids[:, :, None] == jnp.arange(EXPERTS, dtype=jnp.int32)[None, None, :]).astype(jnp.int32)
    slot_index = lax.optimization_barrier(jnp.sum(matches * jnp.cumsum(matches, axis=1), axis=2)) - 1
    block_number = jnp.arange(N_ROW, dtype=jnp.int32)[:, None]
    target_index = ((block_ids * N_ROW + block_number) * CAP + slot_index).reshape(-1).astype(jnp.int32)
    assign_index = jnp.arange(TOKENS * TOP, dtype=jnp.int32)
    assign_table = jnp.full((EXPERTS * N_ROW * CAP,), TOKENS * TOP, jnp.int32).at[target_index].set(assign_index)
    token_table = (assign_table // TOP).astype(jnp.int32)
    gate_weights = gate_levels.reshape(-1).astype(jnp.float32) / 64.0
    token_of = (assign_index // TOP).astype(jnp.int32)
    scaled_grad = (gate_weights[:, None] * cotangent[token_of].astype(jnp.float32)).astype(jnp.bfloat16)
    zero_row = jnp.zeros((1, D), jnp.bfloat16)
    routed_in = jnp.concatenate([normed, zero_row], axis=0)[token_table].reshape(EXPERTS, N_ROW * CAP, D)
    routed_grad = jnp.concatenate([scaled_grad, zero_row], axis=0)[assign_table].reshape(EXPERTS, N_ROW * CAP, D)

    def one_expert(operands):
        inputs, grads, gate_w, up_w, down_w = operands
        pre_gate = jnp.dot(inputs, gate_w.T, preferred_element_type=jnp.float32)
        pre_up = jnp.dot(inputs, up_w.T, preferred_element_type=jnp.float32)
        gate_sigmoid = jax.nn.sigmoid(pre_gate)
        silu_gate = pre_gate * gate_sigmoid
        act = (silu_gate * pre_up).astype(jnp.bfloat16)
        grad_act = jnp.dot(grads, down_w.T, preferred_element_type=jnp.float32)
        grad_gate = (grad_act * pre_up * gate_sigmoid * (1.0 + pre_gate * (1.0 - gate_sigmoid))).astype(jnp.bfloat16)
        grad_up = (grad_act * silu_gate).astype(jnp.bfloat16)
        down_grad = jnp.dot(act.T, grads, preferred_element_type=jnp.float32).astype(jnp.bfloat16)
        gate_grad = jnp.dot(grad_gate.T, inputs, preferred_element_type=jnp.float32).astype(jnp.bfloat16)
        up_grad = jnp.dot(grad_up.T, inputs, preferred_element_type=jnp.float32).astype(jnp.bfloat16)
        slot_count = inputs.shape[0]
        gate_blocks = grad_gate.astype(jnp.float32).reshape(slot_count, N_COL, FBLOCK)
        up_blocks = grad_up.astype(jnp.float32).reshape(slot_count, N_COL, FBLOCK)
        gate_wblocks = gate_w.astype(jnp.float32).reshape(N_COL, FBLOCK, D)
        up_wblocks = up_w.astype(jnp.float32).reshape(N_COL, FBLOCK, D)
        block_terms = jnp.einsum('snf,nfd->nsd', gate_blocks, gate_wblocks) + jnp.einsum('snf,nfd->nsd', up_blocks, up_wblocks)
        rounded = lax.optimization_barrier(block_terms.astype(jnp.bfloat16))
        return (gate_grad, up_grad, down_grad, lax.optimization_barrier(jnp.sum(rounded.astype(jnp.float32), axis=0)))
    d_w_gate, d_w_up, d_w_down, slot_grads = lax.map(one_expert, (routed_in, routed_grad, w_gate, w_up, w_down))
    per_assign = slot_grads.reshape(EXPERTS * N_ROW * CAP, D)[target_index]
    d_normed = lax.optimization_barrier(jnp.sum(per_assign.reshape(TOKENS, TOP, D), axis=1)).astype(jnp.bfloat16)
    return (d_normed, d_w_gate, d_w_up, d_w_down)
```

```python
import math

import jax
import jax.numpy as jnp
from jax import lax
from jax.sharding import PartitionSpec as P

HEAD_DIM = 128
TOP = 6
WINDOW = 1024


def from_behind(x, axis, by):
    devices = lax.axis_size(axis)
    pairs = [(i, i + by) for i in range(devices) if 0 <= i + by < devices]
    return lax.ppermute(x, axis, pairs)


def body(
    resid,
    queries,
    keys,
    values,
    doc_ids,
    norm_gain,
    expert_ids,
    gate_levels,
    w_gate,
    w_up,
    w_down,
    cotangent,
):
    tok_rows, feat_width = queries.shape
    row_index = lax.axis_index("row")
    row_count = lax.axis_size("row")
    reach_count = WINDOW // tok_rows
    key_list = []
    value_list = []
    for distance in range(reach_count, 0, -1):
        moved_keys, moved_values = from_behind((keys, values), "row", distance)
        key_list.append(moved_keys)
        value_list.append(moved_values)
    all_keys = jnp.concatenate(key_list + [keys], axis=0)
    all_values = jnp.concatenate(value_list + [values], axis=0)
    key_total = (reach_count + 1) * tok_rows
    padded_docs = jnp.concatenate([jnp.full((reach_count * tok_rows,), -1, jnp.int32), doc_ids])
    key_docs = lax.dynamic_slice_in_dim(padded_docs, row_index * tok_rows, key_total)
    query_docs = lax.dynamic_slice_in_dim(doc_ids, row_index * tok_rows, tok_rows)
    query_pos = row_index * tok_rows + jnp.arange(tok_rows, dtype=jnp.int32)
    key_pos = (row_index - reach_count) * tok_rows + jnp.arange(key_total, dtype=jnp.int32)
    pos_delta = query_pos[:, None] - key_pos[None, :]
    allowed = (pos_delta >= 0) & (pos_delta < WINDOW) & (query_docs[:, None] == key_docs[None, :])
    heads_here = feat_width // HEAD_DIM
    query_heads = queries.reshape(tok_rows, heads_here, HEAD_DIM)
    key_heads = all_keys.reshape(key_total, heads_here, HEAD_DIM)
    value_heads = all_values.reshape(key_total, heads_here, HEAD_DIM)
    scores = jnp.einsum(
        "qhd,khd->hqk", query_heads, key_heads, preferred_element_type=jnp.float32
    ) * (1.0 / math.sqrt(HEAD_DIM))
    scores = jnp.where(allowed[None], scores, -1e30)
    top_score = jnp.max(scores, axis=2, keepdims=True)
    weights = jnp.exp(scores - top_score)
    probs = (weights / jnp.sum(weights, axis=2, keepdims=True)).astype(jnp.bfloat16)
    attention = jnp.einsum(
        "hqk,khd->qhd", probs, value_heads, preferred_element_type=jnp.float32
    ).reshape(tok_rows, feat_width)
    hidden_in = (resid.astype(jnp.float32) + attention).astype(jnp.bfloat16)
    local_experts = w_gate.shape[0]
    experts_total = local_experts * row_count
    capacity = 4 * tok_rows * TOP // (3 * experts_total)
    flat_ids = expert_ids.reshape(-1)
    order = jnp.arange(flat_ids.shape[0], dtype=jnp.int32)
    earlier = (flat_ids[:, None] == flat_ids[None, :]) & (order[None, :] < order[:, None])
    slot_index = jnp.sum(earlier.astype(jnp.int32), axis=1)
    target_index = flat_ids * capacity + slot_index
    assign_table = (
        jnp.full((experts_total * capacity,), tok_rows * TOP, jnp.int32)
        .at[target_index]
        .set(jnp.arange(tok_rows * TOP, dtype=jnp.int32))
    )
    token_table = assign_table // TOP
    gate_weights = gate_levels.reshape(-1).astype(jnp.float32) / 64.0
    full_hidden, full_grads = (
        lax.all_gather(hidden_in, "col", axis=1, tiled=True),
        lax.all_gather(cotangent, "col", axis=1, tiled=True),
    )
    widened = full_hidden.astype(jnp.float32)
    inv_rms = lax.rsqrt(jnp.mean(widened * widened, axis=1, keepdims=True) + 1e-05)
    normed = (widened * inv_rms * norm_gain[None, :]).astype(jnp.bfloat16)
    feat_count = normed.shape[1]
    zero_row = jnp.zeros((1, feat_count), jnp.bfloat16)
    scaled_grad = (
        gate_weights[:, None] * jnp.repeat(full_grads, TOP, axis=0).astype(jnp.float32)
    ).astype(jnp.bfloat16)
    routed_in = jnp.concatenate([normed, zero_row], axis=0)[token_table].reshape(
        row_count, local_experts, capacity, feat_count
    )
    routed_grad = jnp.concatenate([scaled_grad, zero_row], axis=0)[assign_table].reshape(
        row_count, local_experts, capacity, feat_count
    )
    recv_in, recv_grad = (
        lax.all_to_all(routed_in, "row", split_axis=0, concat_axis=0, tiled=True),
        lax.all_to_all(routed_grad, "row", split_axis=0, concat_axis=0, tiled=True),
    )
    pre_gate = jnp.einsum("secd,efd->secf", recv_in, w_gate, preferred_element_type=jnp.float32)
    pre_up = jnp.einsum("secd,efd->secf", recv_in, w_up, preferred_element_type=jnp.float32)
    gate_sigmoid = jax.nn.sigmoid(pre_gate)
    silu_gate = pre_gate * gate_sigmoid
    act = (silu_gate * pre_up).astype(jnp.bfloat16)
    grad_act = jnp.einsum("secd,efd->secf", recv_grad, w_down, preferred_element_type=jnp.float32)
    grad_gate = (grad_act * pre_up * gate_sigmoid * (1.0 + pre_gate * (1.0 - gate_sigmoid))).astype(
        jnp.bfloat16
    )
    grad_up = (grad_act * silu_gate).astype(jnp.bfloat16)
    d_w_down = jnp.einsum(
        "secf,secd->efd", act, recv_grad, preferred_element_type=jnp.float32
    ).astype(jnp.bfloat16)
    d_w_gate = jnp.einsum(
        "secf,secd->efd", grad_gate, recv_in, preferred_element_type=jnp.float32
    ).astype(jnp.bfloat16)
    d_w_up = jnp.einsum(
        "secf,secd->efd", grad_up, recv_in, preferred_element_type=jnp.float32
    ).astype(jnp.bfloat16)
    block_terms = jnp.einsum(
        "secf,efd->secd", grad_gate, w_gate, preferred_element_type=jnp.float32
    )
    block_terms = block_terms + jnp.einsum(
        "secf,efd->secd", grad_up, w_up, preferred_element_type=jnp.float32
    )
    block_terms = block_terms.astype(jnp.bfloat16)
    returned = lax.all_to_all(block_terms, "row", split_axis=0, concat_axis=0, tiled=True)
    flat_rows = returned.reshape(experts_total * capacity, -1)[target_index]
    d_normed = lax.psum_scatter(
        jnp.sum(flat_rows.astype(jnp.float32).reshape(tok_rows, TOP, -1), axis=1).astype(
            jnp.bfloat16
        ),
        "col",
        scatter_dimension=1,
        tiled=True,
    )
    return (d_normed, d_w_gate, d_w_up, d_w_down)


def solution(mesh):
    return jax.shard_map(
        body,
        mesh=mesh,
        in_specs=(
            P("row", "col"),
            P("row", "col"),
            P("row", "col"),
            P("row", "col"),
            P(),
            P(),
            P("row", None),
            P("row", None),
            P("row", "col", None),
            P("row", "col", None),
            P("row", "col", None),
            P("row", "col"),
        ),
        out_specs=(
            P("row", "col"),
            P("row", "col", None),
            P("row", "col", None),
            P("row", "col", None),
        ),
        check_vma=False,
    )
```

```python
import math

import jax
import jax.numpy as jnp
from jax import lax
from jax.experimental import pallas as pl
from jax.experimental.pallas import tpu as pltpu
from jax.sharding import PartitionSpec as P

HEAD_DIM = 128
WINDOW = 1024
EPS = 1e-05
VMEM = 56 * 2**20
F32, BF16 = jnp.float32, jnp.bfloat16
CORE = 8


def mask_x(k):
    return k << 4


def mask_z(k):
    return k


def mask_y(k):
    return ((k >> 1) << 2) | ((k & 1) << 6)


def swap(x, mask):
    return lax.ppermute(x, ("row", "col"), [(i, i ^ mask) for i in range(128)])


def gather_direct(x, mask):
    return jnp.stack([x, swap(x, mask(1)), swap(x, mask(2)), swap(x, mask(3))])


def gather_ring(x, mask):
    half = x.shape[0] // 2
    one, three = swap(x, mask(1)), swap(x, mask(3))
    low, high = swap(three[:half], mask(1)), swap(one[half:], mask(3))
    return jnp.concatenate([x, one, low, high, three]).reshape(4, *x.shape)


def add(*terms):
    return sum(t.astype(F32) for t in terms).astype(BF16)


def scatter_ring(p, mask):
    half = p.shape[1] // 2
    from_one, from_three = swap(p[2, :half], mask(1)), swap(p[2, half:], mask(3))
    for_one = jnp.concatenate([p[1, :half], add(p[1, half:], from_three)])
    for_three = jnp.concatenate([add(p[3, :half], from_one), p[3, half:]])
    return add(p[0], swap(for_one, mask(1)), swap(for_three, mask(3)))


def scatter_direct(p, mask):
    return add(p[0], swap(p[1], mask(1)), swap(p[2], mask(2)), swap(p[3], mask(3)))


ORDERS = ((mask_z, mask_y, mask_x), (mask_x, mask_z, mask_y), (mask_y, mask_x, mask_z))


def split_rows(rows):
    step = rows // 8
    return ((0, 3 * step), (3 * step, 3 * step), (6 * step, 2 * step))


def gather_tokens(x):
    parts = []
    for (start, size), (first, second, last) in zip(split_rows(x.shape[0]), ORDERS):
        part = gather_direct(x[start : start + size], first)
        part = gather_direct(part, second)
        parts.append(gather_ring(part, last))
    a, b, c = parts
    r, w = x.shape[0], x.shape[1]
    return (
        a.reshape(4, 2, 2, 4, -1, w),
        b.reshape(2, 2, 4, 4, -1, w),
        c.reshape(4, 4, 2, 2, -1, w),
    )


def scatter_tokens(parts):
    outs = []
    for part, (first, second, last) in zip(parts, ORDERS):
        part = part.reshape(4, 4, 4, *part.shape[-2:])
        part = scatter_ring(part, last)
        part = scatter_direct(part, second)
        outs.append(scatter_direct(part, first))
    return jnp.concatenate(outs)


def part_specs(sizes, width):
    a, b, c = sizes
    return [
        pl.BlockSpec((4, None, 2, None, a, width), lambda f, s: (0, f // 4, 0, f % 4, 0, 0)),
        pl.BlockSpec((None, 2, None, 4, b, width), lambda f, s: (f // 4, 0, f % 4, 0, 0, 0)),
        pl.BlockSpec((None, 4, None, 2, c, width), lambda f, s: (f % 4, 0, f // 4, 0, 0, 0)),
    ]


def part_shapes(sizes, width):
    a, b, c = sizes
    return [
        jax.ShapeDtypeStruct((4, 2, 2, 4, a, width), BF16),
        jax.ShapeDtypeStruct((2, 2, 4, 4, b, width), BF16),
        jax.ShapeDtypeStruct((4, 4, 2, 2, c, width), BF16),
    ]


def rows_of(ref):
    return ref[...].reshape(-1, ref.shape[-1])


def dot_nt(a, b):
    return lax.dot_general(a, b, (((1,), (1,)), ((), ())), preferred_element_type=F32)


def dot_nn(a, b):
    return lax.dot_general(a, b, (((1,), (0,)), ((), ())), preferred_element_type=F32)


def weight_spec(w, width):
    return pl.BlockSpec((w.shape[0], w.shape[1], width), lambda f, s: (0, 0, f ^ s[0]))


def whole(shape):
    return pl.BlockSpec(shape, lambda f, s: (0,) * len(shape))


def call(kernel, col, steps, in_specs, out_specs, out_shape, scratch, args, flops, moved):
    return pl.pallas_call(
        kernel,
        out_shape=out_shape,
        grid_spec=pltpu.PrefetchScalarGridSpec(
            num_scalar_prefetch=1,
            grid=(steps,),
            in_specs=in_specs,
            out_specs=out_specs,
            scratch_shapes=scratch,
        ),
        compiler_params=pltpu.CompilerParams(vmem_limit_bytes=VMEM),
        cost_estimate=pl.CostEstimate(flops=flops, bytes_accessed=moved, transcendentals=0),
    )(col, *args)


def attention_kernel(q, own, sib, resid, qdoc, kdoc, qpos, kpos, out):
    width = q.shape[1]
    keys = own.shape[0]
    delta = qpos[...] - kpos[...]
    allowed = (delta >= 0) & (delta < WINDOW) & (qdoc[...] == kdoc[...])
    for h in range(width // HEAD_DIM):
        cols = slice(h * HEAD_DIM, (h + 1) * HEAD_DIM)
        vcols = slice(width + h * HEAD_DIM, width + (h + 1) * HEAD_DIM)
        s = jnp.concatenate([dot_nt(q[:, cols], own[:, cols]), dot_nt(q[:, cols], sib[:, cols])], axis=1)
        s = jnp.where(allowed, s * (1.0 / math.sqrt(HEAD_DIM)), -1e30)
        e = jnp.exp(s - jnp.max(s, axis=1, keepdims=True))
        p = (e / jnp.sum(e, axis=1, keepdims=True)).astype(BF16)
        o = dot_nn(p[:, :keys], own[:, vcols]) + dot_nn(p[:, keys:], sib[:, vcols])
        out[:, cols] = (resid[:, cols].astype(F32) + o).astype(BF16)


def attend(queries, keys, values, resid, doc_ids, row):
    rows, width = queries.shape
    reach = WINDOW // rows
    pair = jnp.concatenate([keys, values], axis=1)
    blocks = []
    for by in range(reach, 0, -2):
        blocks.append(lax.ppermute(pair, "row", [(i, i + by) for i in range(16 - by)]))
    own = jnp.concatenate(blocks + [pair])
    sib = swap(own, CORE)
    padded = jnp.concatenate([jnp.full(((reach + 1) * rows,), -1, jnp.int32), doc_ids])

    def info(r):
        first = r - reach
        docs = lax.dynamic_slice_in_dim(padded, (first + reach + 1) * rows, (reach + 1) * rows)
        pos = first * rows + jnp.arange((reach + 1) * rows, dtype=jnp.int32)
        return docs.reshape(reach + 1, rows)[::2].reshape(1, -1), pos.reshape(reach + 1, rows)[::2].reshape(1, -1)

    (d0, p0), (d1, p1) = info(row), info(row ^ 1)
    kdoc, kpos = jnp.concatenate([d0, d1], axis=1), jnp.concatenate([p0, p1], axis=1)
    kdoc = jnp.where(kpos >= 0, kdoc, -1)
    qdoc = lax.dynamic_slice_in_dim(doc_ids, row * rows, rows)[:, None]
    qpos = row * rows + jnp.arange(rows, dtype=jnp.int32)[:, None]
    return pl.pallas_call(
        attention_kernel,
        out_shape=jax.ShapeDtypeStruct((rows, width), BF16),
        compiler_params=pltpu.CompilerParams(vmem_limit_bytes=VMEM),
        cost_estimate=pl.CostEstimate(flops=4 * rows * width * own.shape[0] * 2, bytes_accessed=4 * own.size, transcendentals=0),
    )(queries, own, sib, resid, qdoc, kdoc, qpos, kpos)


def grad_act_kernel(s, xa, xb, xc, w0, w1, out):
    @pl.when(pl.program_id(0) == 0)
    def _():
        out[...] = jnp.zeros_like(out)

    n = out.shape[1] // 2
    start = 0
    for x in (xa, xb, xc):
        x = rows_of(x)
        span = slice(start, start + x.shape[0])
        start += x.shape[0]
        out[span, :n] += dot_nt(x, rows_of(w0))
        out[span, n:] += dot_nt(x, rows_of(w1))


def hidden_kernel(
    s, xa, xb, xc, wg0, wg1, wu0, wu1, gain, gact, gates, gg_out, gu_out, act_t, gg_t, gu_t, g_acc, u_acc, sq_acc
):
    f = pl.program_id(0)
    tokens, hidden = g_acc.shape
    n = hidden // 2

    @pl.when(f == 0)
    def _():
        g_acc[...] = jnp.zeros_like(g_acc)
        u_acc[...] = jnp.zeros_like(u_acc)
        sq_acc[...] = jnp.zeros_like(sq_acc)

    start = 0
    for x in (xa, xb, xc):
        x = rows_of(x).astype(F32)
        span = slice(start, start + x.shape[0])
        start += x.shape[0]
        sq = x * x
        total = sq[:, :128]
        for j in range(128, x.shape[1], 128):
            total += sq[:, j : j + 128]
        sq_acc[span] += total
        x = (x * gain[...]).astype(BF16)
        g_acc[span, :n] += dot_nt(x, rows_of(wg0))
        g_acc[span, n:] += dot_nt(x, rows_of(wg1))
        u_acc[span, :n] += dot_nt(x, rows_of(wu0))
        u_acc[span, n:] += dot_nt(x, rows_of(wu1))

    @pl.when(f == pl.num_programs(0) - 1)
    def _():
        feats = pl.num_programs(0) * xa.shape[-1]
        expert = lax.broadcasted_iota(jnp.int32, (1, hidden), 1) // (hidden // 4)
        for r in range(0, tokens, 128):
            span = slice(r, r + 128)
            inv = lax.rsqrt(jnp.sum(sq_acc[span], axis=1, keepdims=True) * (1.0 / feats) + EPS)
            gate = jnp.where(
                expert < 2,
                jnp.where(expert == 0, gates[span, 0:1], gates[span, 1:2]),
                jnp.where(expert == 2, gates[span, 2:3], gates[span, 3:4]),
            )
            pre_gate, pre_up = g_acc[span] * inv, u_acc[span] * inv
            sig = jax.nn.sigmoid(pre_gate)
            silu = pre_gate * sig
            grad = gact[span] * gate
            gg = grad * pre_up * sig * (1.0 + pre_gate * (1.0 - sig))
            gu = grad * silu
            gg_out[span] = gg.astype(BF16)
            gu_out[span] = gu.astype(BF16)
            act_t[:, span] = (silu * pre_up * gate).T.astype(BF16)
            gg_t[:, span] = (gg * inv).T.astype(BF16)
            gu_t[:, span] = (gu * inv).T.astype(BF16)


def piece_kernel(s, gg, gu, wg0, wg1, wu0, wu1, oa, ob, oc):
    n = gg.shape[1] // 2
    start = 0
    for o in (oa, ob, oc):
        size = o.shape[0] * o.shape[1] * o.shape[2]
        span = slice(start, start + size)
        start += size
        out = dot_nn(gg[span, :n], rows_of(wg0)) + dot_nn(gg[span, n:], rows_of(wg1))
        out += dot_nn(gu[span, :n], rows_of(wu0)) + dot_nn(gu[span, n:], rows_of(wu1))
        o[...] = out.astype(BF16).reshape(o.shape)


def weight_grad_kernel(with_more, s, gain, *refs):
    xs, cs = refs[:3], refs[3:6]
    act_t, gg_t, gu_t = refs[6:9]
    more = refs[9:12] if with_more else (None,) * 3
    dg, du, dd = refs[-3:]
    for lhs, data, scale, extra, out in (
        (gg_t, xs, gain, more[0], dg),
        (gu_t, xs, gain, more[1], du),
        (act_t, cs, None, more[2], dd),
    ):
        start = 0
        total = None
        for x in data:
            x = rows_of(x)
            term = dot_nn(lhs[:, start : start + x.shape[0]], x)
            start += x.shape[0]
            total = term if total is None else total + term
        if scale is not None:
            total = total * scale[...]
        if extra is not None:
            total = total + rows_of(extra).astype(F32)
        out[...] = total.astype(BF16).reshape(out.shape)


def body(
    resid, queries, keys, values, doc_ids, norm_gain, expert_ids, gate_levels, w_gate, w_up, w_down, cotangent
):
    rows, width = queries.shape
    row, col = lax.axis_index("row"), lax.axis_index("col")
    experts, inner, feats = w_gate.shape
    steps = feats // width
    hidden = 2 * experts * inner
    tokens = 8 * rows
    sizes = [size for _, size in split_rows(rows)]
    here = jnp.reshape(col, (1,)).astype(jnp.int32)

    hidden_in = attend(queries, keys, values, resid, doc_ids, row)
    ids = jnp.arange(16 * experts, dtype=jnp.int32)
    table = jnp.sum(
        jnp.where(expert_ids[:, :, None] == ids, gate_levels[:, :, None].astype(F32) / 64.0, 0.0), axis=1
    ).astype(BF16)
    table = gather_direct(table, mask_x)
    table = jnp.stack([table, swap(table, mask_y(1))])
    gates = []
    for (start, size), swapped in zip(split_rows(rows), (True, False, True)):
        part = table[:, :, start : start + size]
        gates.append((jnp.swapaxes(part, 0, 1) if swapped else part).reshape(8 * size, -1))
    gates = jnp.concatenate(gates)
    gates = jnp.concatenate(
        [lax.dynamic_slice_in_dim(gates, experts * r, experts, axis=1) for r in (row, row ^ 1)], axis=1
    ).astype(F32)

    sib_down, sib_gate, sib_up = swap(w_down, CORE), swap(w_gate, CORE), swap(w_up, CORE)
    cot = gather_tokens(cotangent)
    x = gather_tokens(hidden_in)
    gain = norm_gain.reshape(1, feats)

    xs = part_specs(sizes, width)
    ws = weight_spec(w_gate, width)
    gain_spec = pl.BlockSpec((1, width), lambda f, s: (0, f ^ s[0]))
    one = 2 * tokens * hidden * feats
    grad_act = call(
        grad_act_kernel, here, steps, xs + [ws] * 2, whole((tokens, hidden)),
        jax.ShapeDtypeStruct((tokens, hidden), F32), [], (*cot, w_down, sib_down), one, 2 * tokens * feats * 2,
    )
    flat = jax.ShapeDtypeStruct((tokens, hidden), BF16)
    turned = jax.ShapeDtypeStruct((hidden, tokens), BF16)
    gg, gu, act_t, gg_t, gu_t = call(
        hidden_kernel, here, steps,
        xs + [ws] * 4 + [gain_spec, whole((tokens, hidden)), whole((tokens, 4))],
        [whole((tokens, hidden))] * 2 + [whole((hidden, tokens))] * 3,
        [flat, flat, turned, turned, turned],
        [pltpu.VMEM((tokens, hidden), F32), pltpu.VMEM((tokens, hidden), F32), pltpu.VMEM((tokens, 128), F32)],
        (*x, w_gate, sib_gate, w_up, sib_up, gain, grad_act, gates), 2 * one, 4 * tokens * feats,
    )
    pieces = call(
        piece_kernel, here, steps, [whole((tokens, hidden))] * 2 + [ws] * 4, xs, part_shapes(sizes, width), [],
        (gg, gu, w_gate, sib_gate, w_up, sib_up), 2 * one, 4 * tokens * feats,
    )
    d_normed = scatter_tokens(pieces)

    def weight_grads(which, more):
        half = pl.BlockSpec((hidden // 2, tokens), lambda f, s: (which, 0))
        return call(
            lambda *refs: weight_grad_kernel(bool(more), *refs), here, steps,
            [gain_spec] + xs * 2 + [half] * 3 + [ws] * len(more), [ws] * 3,
            [jax.ShapeDtypeStruct(w_gate.shape, BF16)] * 3, [],
            (gain, *x, *cot, act_t, gg_t, gu_t, *more), 3 * one // 2, 4 * tokens * feats,
        )

    sent = weight_grads(1, ())
    d_gate, d_up, d_down = weight_grads(0, tuple(swap(d, CORE) for d in sent))
    return (d_normed, d_gate, d_up, d_down)


def solution(mesh):
    tile, split3 = P("row", "col"), P("row", "col", None)
    return jax.shard_map(
        body,
        mesh=mesh,
        in_specs=(tile, tile, tile, tile, P(), P(), P("row", None), P("row", None), split3, split3, split3, tile),
        out_specs=(tile, split3, split3, split3),
        check_vma=False,
    )
```

```python
import math

import jax
import jax.numpy as jnp
from jax import lax
from jax.experimental import pallas as pl
from jax.experimental.pallas import tpu as pltpu
from jax.sharding import PartitionSpec as P

HEAD_DIM = 128
WINDOW = 1024
EPS = 1e-05
VMEM = 56 * 2**20
F32, BF16 = jnp.float32, jnp.bfloat16
CORE = 8


def mask_x(k):
    return k << 4


def mask_z(k):
    return k


def mask_y(k):
    return ((k >> 1) << 2) | ((k & 1) << 6)


def swap(x, mask):
    return lax.ppermute(x, ("row", "col"), [(i, i ^ mask) for i in range(128)])


def gather_direct(x, mask):
    return jnp.stack([x, swap(x, mask(1)), swap(x, mask(2)), swap(x, mask(3))])


def gather_ring(x, mask):
    half = x.shape[0] // 2
    one, three = swap(x, mask(1)), swap(x, mask(3))
    low, high = swap(three[:half], mask(1)), swap(one[half:], mask(3))
    return jnp.concatenate([x, one, low, high, three]).reshape(4, *x.shape)


def add(*terms):
    return sum(t.astype(F32) for t in terms).astype(BF16)


def scatter_ring(p, mask, tie):
    half = p.shape[1] // 2
    from_one, from_three = swap(p[2, :half], mask(1)), swap(p[2, half:], mask(3))
    from_one, from_three = tie(from_one, from_three)
    for_one = jnp.concatenate([p[1, :half], add(p[1, half:], from_three)])
    for_three = jnp.concatenate([add(p[3, :half], from_one), p[3, half:]])
    return add(p[0], swap(for_one, mask(1)), swap(for_three, mask(3)))


def scatter_direct(p, mask):
    return add(p[0], swap(p[1], mask(1)), swap(p[2], mask(2)), swap(p[3], mask(3)))


ORDERS = ((mask_z, mask_y, mask_x), (mask_x, mask_z, mask_y), (mask_y, mask_x, mask_z))


def split_rows(rows):
    step = rows // 8
    return ((0, 3 * step), (3 * step, 3 * step), (6 * step, 2 * step))


def gather_tokens(x):
    parts = []
    for (start, size), (first, second, last) in zip(split_rows(x.shape[0]), ORDERS):
        part = gather_direct(x[start : start + size], first)
        part = gather_direct(part, second)
        parts.append(gather_ring(part, last))
    a, b, c = parts
    r, w = x.shape[0], x.shape[1]
    return (
        a.reshape(4, 2, 2, 4, -1, w),
        b.reshape(2, 2, 4, 4, -1, w),
        c.reshape(4, 4, 2, 2, -1, w),
    )


def scatter_part(part, order, tie):
    first, second, last = order
    part = part.reshape(4, 4, 4, *part.shape[-2:])
    return scatter_direct(scatter_direct(scatter_ring(part, last, tie), second), first)


def part_specs(sizes, width, side=0):
    a, b, c = sizes
    return [
        pl.BlockSpec((4, None, 2, 2, a, width), lambda f, s: (0, f // 2, 0, f % 2, 0, side)),
        pl.BlockSpec((None, 2, 2, 4, b, width), lambda f, s: (f // 2, 0, f % 2, 0, 0, side)),
        pl.BlockSpec((2, 4, None, 2, c, width), lambda f, s: (f % 2, 0, f // 2, 0, 0, side)),
    ]


PAIR_AXES = (2, 1, 0)


def pair_at(axis, i):
    return (slice(None),) * axis + (i,)


def pair_rows(ref, axis, odd):
    sides = [ref[pair_at(axis, i)].reshape(-1, ref.shape[-1]) for i in (odd, 1 - odd)]
    return jnp.concatenate(sides, axis=1)


def stacked(*refs):
    return jnp.concatenate([rows_of(r) for r in refs])


def part_shapes(sizes, width):
    a, b, c = sizes
    return [
        jax.ShapeDtypeStruct((4, 2, 2, 4, a, width), BF16),
        jax.ShapeDtypeStruct((2, 2, 4, 4, b, width), BF16),
        jax.ShapeDtypeStruct((4, 4, 2, 2, c, width), BF16),
    ]


def rows_of(ref):
    return ref[...].reshape(-1, ref.shape[-1])


def dot_nt(a, b):
    return lax.dot_general(a, b, (((1,), (1,)), ((), ())), preferred_element_type=F32)


def dot_nn(a, b):
    return lax.dot_general(a, b, (((1,), (0,)), ((), ())), preferred_element_type=F32)


def weight_spec(w, width):
    return pl.BlockSpec((w.shape[0], w.shape[1], 2 * width), lambda f, s: (0, 0, f ^ (s[0] // 2)))


def whole(shape):
    return pl.BlockSpec(shape, lambda f, s: (0,) * len(shape))


def call(kernel, col, steps, in_specs, out_specs, out_shape, scratch, args, flops, moved):
    return pl.pallas_call(
        kernel,
        out_shape=out_shape,
        grid_spec=pltpu.PrefetchScalarGridSpec(
            num_scalar_prefetch=1,
            grid=(steps,),
            in_specs=in_specs,
            out_specs=out_specs,
            scratch_shapes=scratch,
        ),
        compiler_params=pltpu.CompilerParams(vmem_limit_bytes=VMEM),
        cost_estimate=pl.CostEstimate(flops=flops, bytes_accessed=moved, transcendentals=0),
    )(col, *args)


def attention_kernel(q, own, sib, resid, cot, qdoc, kdoc, qpos, kpos, out):
    width = q.shape[1]
    out[:, :width] = cot[...]
    keys = own.shape[0]
    delta = qpos[...] - kpos[...]
    allowed = (delta >= 0) & (delta < WINDOW) & (qdoc[...] == kdoc[...])
    for h in range(width // HEAD_DIM):
        cols = slice(h * HEAD_DIM, (h + 1) * HEAD_DIM)
        vcols = slice(width + h * HEAD_DIM, width + (h + 1) * HEAD_DIM)
        s = jnp.concatenate([dot_nt(q[:, cols], own[:, cols]), dot_nt(q[:, cols], sib[:, cols])], axis=1)
        s = jnp.where(allowed, s * (1.0 / math.sqrt(HEAD_DIM)), -1e30)
        e = jnp.exp(s - jnp.max(s, axis=1, keepdims=True))
        p = (e / jnp.sum(e, axis=1, keepdims=True)).astype(BF16)
        o = dot_nn(p[:, :keys], own[:, vcols]) + dot_nn(p[:, keys:], sib[:, vcols])
        out[:, vcols] = (resid[:, cols].astype(F32) + o).astype(BF16)


def attend(queries, keys, values, resid, cotangent, doc_ids, row):
    rows, width = queries.shape
    reach = WINDOW // rows
    pair = jnp.concatenate([keys, values], axis=1)
    blocks = []
    for by in range(reach, 0, -2):
        blocks.append(lax.ppermute(pair, "row", [(i, i + by) for i in range(16 - by)]))
    own = jnp.concatenate(blocks + [pair])
    sib = swap(own, CORE)
    padded = jnp.concatenate([jnp.full(((reach + 1) * rows,), -1, jnp.int32), doc_ids])

    def info(r):
        first = r - reach
        docs = lax.dynamic_slice_in_dim(padded, (first + reach + 1) * rows, (reach + 1) * rows)
        pos = first * rows + jnp.arange((reach + 1) * rows, dtype=jnp.int32)
        return docs.reshape(reach + 1, rows)[::2].reshape(1, -1), pos.reshape(reach + 1, rows)[::2].reshape(1, -1)

    (d0, p0), (d1, p1) = info(row), info(row ^ 1)
    kdoc, kpos = jnp.concatenate([d0, d1], axis=1), jnp.concatenate([p0, p1], axis=1)
    kdoc = jnp.where(kpos >= 0, kdoc, -1)
    qdoc = lax.dynamic_slice_in_dim(doc_ids, row * rows, rows)[:, None]
    qpos = row * rows + jnp.arange(rows, dtype=jnp.int32)[:, None]
    return pl.pallas_call(
        attention_kernel,
        out_shape=jax.ShapeDtypeStruct((rows, 2 * width), BF16),
        compiler_params=pltpu.CompilerParams(vmem_limit_bytes=VMEM),
        cost_estimate=pl.CostEstimate(flops=4 * rows * width * own.shape[0] * 2, bytes_accessed=4 * own.size, transcendentals=0),
    )(queries, own, sib, resid, cotangent, qdoc, kdoc, qpos, kpos)


def hidden_kernel(
    s, ca, cb, cc, xa, xb, xc, wg0, wg1, wu0, wu1, wd0, wd1, gain, gates,
    gg_out, gu_out, act_t, gg_t, gu_t, g_acc, u_acc, d_acc, sq_acc
):
    f = pl.program_id(0)
    tokens, hidden = g_acc.shape
    odd = s[0] % 2

    def products(first):
        start = 0
        for axis, c, x in zip(PAIR_AXES, (ca, cb, cc), (xa, xb, xc)):
            x = pair_rows(x, axis, odd).astype(F32)
            span = slice(start, start + x.shape[0])
            start += x.shape[0]
            sq = x * x
            total = sq[:, :128]
            for j in range(128, x.shape[1], 128):
                total += sq[:, j : j + 128]
            x = (x * gain[...]).astype(BF16)
            for acc, value in (
                (sq_acc, total),
                (g_acc, dot_nt(x, stacked(wg0, wg1))),
                (u_acc, dot_nt(x, stacked(wu0, wu1))),
                (d_acc, dot_nt(pair_rows(c, axis, odd), stacked(wd0, wd1))),
            ):
                acc[span] = value if first else acc[span] + value

    @pl.when(f == 0)
    def _():
        products(True)

    @pl.when(f > 0)
    def _():
        products(False)

    @pl.when(f == pl.num_programs(0) - 1)
    def _():
        feats = pl.num_programs(0) * 2 * xa.shape[-1]
        expert = lax.broadcasted_iota(jnp.int32, (1, hidden), 1) // (hidden // 4)
        for r in range(0, tokens, 128):
            span = slice(r, r + 128)
            inv = lax.rsqrt(jnp.sum(sq_acc[span], axis=1, keepdims=True) * (1.0 / feats) + EPS)
            gate = jnp.where(
                expert < 2,
                jnp.where(expert == 0, gates[span, 0:1], gates[span, 1:2]),
                jnp.where(expert == 2, gates[span, 2:3], gates[span, 3:4]),
            )
            pre_gate, pre_up = g_acc[span] * inv, u_acc[span] * inv
            sig = jax.nn.sigmoid(pre_gate)
            silu = pre_gate * sig
            grad = d_acc[span] * gate
            gg = grad * pre_up * sig * (1.0 + pre_gate * (1.0 - sig))
            gu = grad * silu
            gg_out[span] = gg.astype(BF16)
            gu_out[span] = gu.astype(BF16)
            act_t[:, span] = (silu * pre_up * gate).T.astype(BF16)
            gg_t[:, span] = (gg * inv).T.astype(BF16)
            gu_t[:, span] = (gu * inv).T.astype(BF16)


def piece_kernel(axis, s, gg, gu, wg0, wg1, wu0, wu1, o):
    odd = s[0] % 2
    width = o.shape[-1]
    out = dot_nn(gg[...], stacked(wg0, wg1)) + dot_nn(gu[...], stacked(wu0, wu1))
    for i, at in enumerate((odd, 1 - odd)):
        at = pair_at(axis, at)
        o[at] = out[:, i * width : (i + 1) * width].astype(BF16).reshape(o.at[at].shape)


def weight_grad_kernel(with_more, s, gain, *refs):
    xs, cs = refs[:3], refs[3:6]
    act_t, gg_t, gu_t = refs[6:9]
    more = refs[9:12] if with_more else (None,) * 3
    dg, du, dd = refs[-3:]
    odd = s[0] % 2
    for lhs, data, scale, extra, out in (
        (gg_t, xs, gain, more[0], dg),
        (gu_t, xs, gain, more[1], du),
        (act_t, cs, None, more[2], dd),
    ):
        rows = jnp.concatenate([pair_rows(x, axis, odd) for axis, x in zip(PAIR_AXES, data)])
        total = dot_nn(lhs[...], rows)
        if scale is not None:
            total = total * scale[...]
        if extra is not None:
            total = total + rows_of(extra).astype(F32)
        out[...] = total.astype(BF16).reshape(out.shape)


def body(
    resid, queries, keys, values, doc_ids, norm_gain, expert_ids, gate_levels, w_gate, w_up, w_down, cotangent
):
    rows, width = queries.shape
    row, col = lax.axis_index("row"), lax.axis_index("col")
    experts, inner, feats = w_gate.shape
    steps = feats // width // 2
    hidden = 2 * experts * inner
    tokens = 8 * rows
    sizes = [size for _, size in split_rows(rows)]
    here = jnp.reshape(col, (1,)).astype(jnp.int32)

    paired = attend(queries, keys, values, resid, cotangent, doc_ids, row)
    ids = jnp.arange(16 * experts, dtype=jnp.int32)
    table = jnp.sum(
        jnp.where(expert_ids[:, :, None] == ids, gate_levels[:, :, None].astype(F32) / 64.0, 0.0), axis=1
    ).astype(BF16)
    table = gather_direct(table, mask_x)
    table = jnp.stack([table, swap(table, mask_y(1))])
    gates = []
    for (start, size), swapped in zip(split_rows(rows), (True, False, True)):
        part = table[:, :, start : start + size]
        gates.append((jnp.swapaxes(part, 0, 1) if swapped else part).reshape(8 * size, -1))
    gates = jnp.concatenate(gates)
    gates = jnp.concatenate(
        [lax.dynamic_slice_in_dim(gates, experts * r, experts, axis=1) for r in (row, row ^ 1)], axis=1
    ).astype(F32)

    sib_down, sib_gate, sib_up = swap(w_down, CORE), swap(w_gate, CORE), swap(w_up, CORE)
    x = gather_tokens(paired)
    gain = norm_gain.reshape(1, feats)

    cs, xs = part_specs(sizes, width, 0), part_specs(sizes, width, 1)
    ws = weight_spec(w_gate, width)
    gain_spec = pl.BlockSpec((1, 2 * width), lambda f, s: (0, f ^ (s[0] // 2)))
    one = 2 * tokens * hidden * feats
    flat = jax.ShapeDtypeStruct((tokens, hidden), BF16)
    turned = jax.ShapeDtypeStruct((hidden, tokens), BF16)
    kept = pl.BlockSpec(memory_space=pltpu.VMEM)
    gg, gu, act_t, gg_t, gu_t = call(
        hidden_kernel, here, steps,
        cs + xs + [ws] * 6 + [gain_spec, whole((tokens, 4))],
        [kept] * 5, [flat, flat, turned, turned, turned],
        [pltpu.VMEM((tokens, hidden), F32)] * 3 + [pltpu.VMEM((tokens, 128), F32)],
        (*x, *x, w_gate, sib_gate, w_up, sib_up, w_down, sib_down, gain, gates), 3 * one, 8 * tokens * feats,
    )
    pieces = []
    outs = part_specs(sizes, width)
    for i, (start, size) in enumerate(split_rows(rows)):
        rows_spec = pl.BlockSpec((8 * size, hidden), lambda f, s, at=start // size: (at, 0))
        pieces.append(
            call(
                lambda *refs, axis=PAIR_AXES[i]: piece_kernel(axis, *refs), here, steps,
                [rows_spec] * 2 + [ws] * 4, outs[i], part_shapes(sizes, width)[i], [],
                (gg, gu, w_gate, sib_gate, w_up, sib_up), 2 * one * size // rows, 8 * hidden * feats,
            )
        )

    def weight_grads(which, more):
        half = pl.BlockSpec((hidden // 2, tokens), lambda f, s: (which, 0))
        return call(
            lambda *refs: weight_grad_kernel(bool(more), *refs), here, steps,
            [gain_spec] + xs + cs + [half] * 3 + [ws] * len(more), [ws] * 3,
            [jax.ShapeDtypeStruct(w_gate.shape, BF16)] * 3, [],
            (gain, *x, *x, act_t, gg_t, gu_t, *more), 3 * one // 2, 8 * tokens * feats,
        )

    sent = weight_grads(1, ())
    sums = []
    for part, order in zip(pieces, ORDERS):
        sums.append(scatter_part(part, order, lambda a, b: lax.optimization_barrier((a, b, sent[0][:1, :1, :128]))[:2]))
    d_normed = jnp.concatenate(sums)
    d_gate, d_up, d_down = weight_grads(0, tuple(swap(d, CORE) for d in sent))
    return (d_normed, d_gate, d_up, d_down)


def solution(mesh):
    tile, split3 = P("row", "col"), P("row", "col", None)
    return jax.shard_map(
        body,
        mesh=mesh,
        in_specs=(tile, tile, tile, tile, P(), P(), P("row", None), P("row", None), split3, split3, split3, tile),
        out_specs=(tile, split3, split3, split3),
        check_vma=False,
    )
```

```python
import math

import jax
import jax.numpy as jnp
from jax import lax
from jax.experimental import pallas as pl
from jax.experimental.pallas import tpu as pltpu
from jax.sharding import PartitionSpec as P

HEAD_DIM = 128
WINDOW = 1024
EPS = 1e-05
VMEM = 56 * 2**20
F32, BF16 = jnp.float32, jnp.bfloat16
def mask_core(i):
    return 8


def mask_x(k):
    return lambda i: (k ^ (k & 1) * (i >> 2 & 2)) << 4


def mask_z(k):
    return lambda i: k


def mask_y(k):
    return lambda i: ((k >> 1) << 2) | ((k & 1) << 6)


def swap(x, mask):
    return lax.ppermute(x, ("row", "col"), [(i, i ^ mask(i)) for i in range(128)])


tied = lax.optimization_barrier


def fetch(x, mask):
    return [x, swap(x, mask(1)), swap(x, mask(2)), swap(x, mask(3))]


def add(*terms):
    return sum(t.astype(F32) for t in terms).astype(BF16)


ORDERS = ((mask_z, mask_y, mask_x), (mask_x, mask_z, mask_y), (mask_y, mask_x, mask_z))


def split_rows(rows):
    step = rows // 8
    return ((0, 2 * step), (2 * step, 3 * step), (5 * step, 3 * step))


def gather_tokens(x):
    width = x.shape[1]
    parts = [x[start : start + size] for start, size in split_rows(x.shape[0])]
    for stage in (0, 1):
        got = tied([fetch(part, order[stage]) for part, order in zip(parts, ORDERS)])
        parts = [jnp.stack(g) for g in got]
    pairs = []
    for i, (part, order) in enumerate(zip(parts, ORDERS)):
        one = swap(part, order[2](1))
        again = tied((part, one))[0] if i == 0 else part
        pairs.append((one, swap(again, order[2](3))))
    pairs = tied(pairs)
    wholes = []
    for part, (one, three), (_, _, last) in zip(parts, pairs, ORDERS):
        wholes.append([part, one, swap(three[:2], last(1)), swap(one[2:], last(3)), three])
    a, b, c = [jnp.concatenate(w) for w in wholes]
    a = a.reshape(4, 2, 2, 4, -1, width)
    b = b.reshape(2, 2, 4, 4, -1, width)
    c = c.reshape(4, 4, 2, 2, -1, width)
    return (a, b, c)


def scatter_first(p, order):
    p = p.reshape(4, 4, 4, *p.shape[-2:])
    return p, swap(p[2, :2], order[2](1)), swap(p[2, 2:], order[2](3))


def scatter_next(p, from_one, from_three):
    for_one = jnp.concatenate([p[1, :2], add(p[1, 2:], from_three)])
    for_three = jnp.concatenate([add(p[3, :2], from_one), p[3, 2:]])
    return p[0], for_one, for_three


def send_pair(p, order):
    mine, for_one, for_three = p
    return mine, swap(for_one, order[2](1)), swap(for_three, order[2](3))


def send_three(p, mask):
    return p[0], swap(p[1], mask(1)), swap(p[2], mask(2)), swap(p[3], mask(3))


def part_specs(sizes, width, side=0):
    a, b, c = sizes
    return [
        pl.BlockSpec((4, None, 2, 2, a, width), lambda f, s: (0, f // 2, 0, f % 2, 0, side)),
        pl.BlockSpec((None, 2, 2, 4, b, width), lambda f, s: (f // 2, 0, f % 2, 0, 0, side)),
        pl.BlockSpec((2, 4, None, 2, c, width), lambda f, s: (f % 2, 0, f // 2, 0, 0, side)),
    ]


PAIR_AXES = (2, 1, 0)


def pair_at(axis, i):
    return (slice(None),) * axis + (i,)


def pair_rows(ref, axis, odd):
    sides = [ref[pair_at(axis, i)].reshape(-1, ref.shape[-1]) for i in (odd, 1 - odd)]
    return jnp.concatenate(sides, axis=1)


def stacked(*refs):
    return jnp.concatenate([rows_of(r) for r in refs])


def part_shapes(sizes, width):
    a, b, c = sizes
    return [
        jax.ShapeDtypeStruct((4, 2, 2, 4, a, width), BF16),
        jax.ShapeDtypeStruct((2, 2, 4, 4, b, width), BF16),
        jax.ShapeDtypeStruct((4, 4, 2, 2, c, width), BF16),
    ]


def rows_of(ref):
    return ref[...].reshape(-1, ref.shape[-1])


def dot_nt(a, b):
    return lax.dot_general(a, b, (((1,), (1,)), ((), ())), preferred_element_type=F32)


def dot_nn(a, b):
    return lax.dot_general(a, b, (((1,), (0,)), ((), ())), preferred_element_type=F32)


def weight_spec(w, width):
    return pl.BlockSpec((w.shape[0], w.shape[1], 2 * width), lambda f, s: (0, 0, f ^ (s[0] // 2)))


def whole(shape):
    return pl.BlockSpec(shape, lambda f, s: (0,) * len(shape))


def call(kernel, col, steps, in_specs, out_specs, out_shape, scratch, args, flops, moved):
    return pl.pallas_call(
        kernel,
        out_shape=out_shape,
        grid_spec=pltpu.PrefetchScalarGridSpec(
            num_scalar_prefetch=1,
            grid=(steps,),
            in_specs=in_specs,
            out_specs=out_specs,
            scratch_shapes=scratch,
        ),
        compiler_params=pltpu.CompilerParams(vmem_limit_bytes=VMEM),
        cost_estimate=pl.CostEstimate(flops=flops, bytes_accessed=moved, transcendentals=0),
    )(col, *args)


def attention_kernel(q, own, sib, resid, cot, qdoc, kdoc, qpos, kpos, out):
    width = q.shape[1]
    out[:, :width] = cot[...]
    keys = own.shape[0]
    delta = qpos[...] - kpos[...]
    allowed = (delta >= 0) & (delta < WINDOW) & (qdoc[...] == kdoc[...])
    for h in range(width // HEAD_DIM):
        cols = slice(h * HEAD_DIM, (h + 1) * HEAD_DIM)
        vcols = slice(width + h * HEAD_DIM, width + (h + 1) * HEAD_DIM)
        s = jnp.concatenate([dot_nt(q[:, cols], own[:, cols]), dot_nt(q[:, cols], sib[:, cols])], axis=1)
        s = jnp.where(allowed, s * (1.0 / math.sqrt(HEAD_DIM)), -1e30)
        e = jnp.exp(s - jnp.max(s, axis=1, keepdims=True))
        p = (e / jnp.sum(e, axis=1, keepdims=True)).astype(BF16)
        o = dot_nn(p[:, :keys], own[:, vcols]) + dot_nn(p[:, keys:], sib[:, vcols])
        out[:, vcols] = (resid[:, cols].astype(F32) + o).astype(BF16)


def attend(queries, keys, values, resid, cotangent, doc_ids, row, weights, table):
    rows, width = queries.shape
    reach = WINDOW // rows
    pair = jnp.concatenate([keys, values], axis=1)
    blocks = []
    for by in range(reach, 0, -2):
        blocks.append(lax.ppermute(pair, "row", [(i, i + by) for i in range(16 - by)]))
    siblings = []
    for w in weights:
        w = tied((w, siblings))[0]
        siblings.append(swap(w, mask_core))
    blocks, siblings, table = tied((blocks, siblings, table))
    own = jnp.concatenate(blocks + [pair])
    sib = swap(own, mask_core)
    padded = jnp.concatenate([jnp.full(((reach + 1) * rows,), -1, jnp.int32), doc_ids])

    def info(r):
        first = r - reach
        docs = lax.dynamic_slice_in_dim(padded, (first + reach + 1) * rows, (reach + 1) * rows)
        pos = first * rows + jnp.arange((reach + 1) * rows, dtype=jnp.int32)
        return docs.reshape(reach + 1, rows)[::2].reshape(1, -1), pos.reshape(reach + 1, rows)[::2].reshape(1, -1)

    (d0, p0), (d1, p1) = info(row), info(row ^ 1)
    kdoc, kpos = jnp.concatenate([d0, d1], axis=1), jnp.concatenate([p0, p1], axis=1)
    kdoc = jnp.where(kpos >= 0, kdoc, -1)
    qdoc = lax.dynamic_slice_in_dim(doc_ids, row * rows, rows)[:, None]
    qpos = row * rows + jnp.arange(rows, dtype=jnp.int32)[:, None]
    out = pl.pallas_call(
        attention_kernel,
        out_shape=jax.ShapeDtypeStruct((rows, 2 * width), BF16),
        compiler_params=pltpu.CompilerParams(vmem_limit_bytes=VMEM),
        cost_estimate=pl.CostEstimate(flops=4 * rows * width * own.shape[0] * 2, bytes_accessed=4 * own.size, transcendentals=0),
    )(queries, own, sib, resid, cotangent, qdoc, kdoc, qpos, kpos)
    return out, siblings, table


def hidden_kernel(
    s, ca, cb, cc, xa, xb, xc, wg0, wg1, wu0, wu1, wd0, wd1, gain, gates,
    gg_out, gu_out, act_t, gg_t, gu_t, g_acc, u_acc, d_acc, sq_acc
):
    f = pl.program_id(0)
    tokens, hidden = g_acc.shape
    odd = s[0] % 2

    def products(first):
        start = 0
        for axis, c, x in zip(PAIR_AXES, (ca, cb, cc), (xa, xb, xc)):
            x = pair_rows(x, axis, odd).astype(F32)
            span = slice(start, start + x.shape[0])
            start += x.shape[0]
            sq = x * x
            total = sq[:, :128]
            for j in range(128, x.shape[1], 128):
                total += sq[:, j : j + 128]
            x = (x * gain[...]).astype(BF16)
            for acc, value in (
                (sq_acc, total),
                (g_acc, dot_nt(x, stacked(wg0, wg1))),
                (u_acc, dot_nt(x, stacked(wu0, wu1))),
                (d_acc, dot_nt(pair_rows(c, axis, odd), stacked(wd0, wd1))),
            ):
                acc[span] = value if first else acc[span] + value

    @pl.when(f == 0)
    def _():
        products(True)

    @pl.when(f > 0)
    def _():
        products(False)

    @pl.when(f == pl.num_programs(0) - 1)
    def _():
        feats = pl.num_programs(0) * 2 * xa.shape[-1]
        expert = lax.broadcasted_iota(jnp.int32, (1, hidden), 1) // (hidden // 4)
        for r in range(0, tokens, 128):
            span = slice(r, r + 128)
            inv = lax.rsqrt(jnp.sum(sq_acc[span], axis=1, keepdims=True) * (1.0 / feats) + EPS)
            gate = jnp.where(
                expert < 2,
                jnp.where(expert == 0, gates[span, 0:1], gates[span, 1:2]),
                jnp.where(expert == 2, gates[span, 2:3], gates[span, 3:4]),
            )
            pre_gate, pre_up = g_acc[span] * inv, u_acc[span] * inv
            sig = jax.nn.sigmoid(pre_gate)
            silu = pre_gate * sig
            grad = d_acc[span] * gate
            gg = grad * pre_up * sig * (1.0 + pre_gate * (1.0 - sig))
            gu = grad * silu
            gg_out[span] = gg.astype(BF16)
            gu_out[span] = gu.astype(BF16)
            act_t[:, span] = (silu * pre_up * gate).T.astype(BF16)
            gg_t[:, span] = (gg * inv).T.astype(BF16)
            gu_t[:, span] = (gu * inv).T.astype(BF16)


def piece_kernel(axis, span, s, gg, gu, wg0, wg1, wu0, wu1, o):
    odd = s[0] % 2
    width = o.shape[-1]
    out = dot_nn(gg[span], stacked(wg0, wg1)) + dot_nn(gu[span], stacked(wu0, wu1))
    for i, at in enumerate((odd, 1 - odd)):
        at = pair_at(axis, at)
        o[at] = out[:, i * width : (i + 1) * width].astype(BF16).reshape(o.at[at].shape)


def weight_grad_kernel(with_more, s, gain, *refs):
    xs, cs = refs[:3], refs[3:6]
    act_t, gg_t, gu_t = refs[6:9]
    more = refs[9] if with_more else None
    dg, du, dd = refs[-3:] if with_more else [refs[-1].at[i] for i in range(3)]
    odd = s[0] % 2
    for lhs, data, scale, extra, out in (
        (gg_t, xs, gain, 0, dg),
        (gu_t, xs, gain, 1, du),
        (act_t, cs, None, 2, dd),
    ):
        rows = jnp.concatenate([pair_rows(x, axis, odd) for axis, x in zip(PAIR_AXES, data)])
        total = dot_nn(lhs[...], rows)
        if scale is not None:
            total = total * scale[...]
        if with_more:
            total = total + more[extra].reshape(total.shape).astype(F32)
        out[...] = total.astype(BF16).reshape(out.shape)


def body(
    resid, queries, keys, values, doc_ids, norm_gain, expert_ids, gate_levels, w_gate, w_up, w_down, cotangent
):
    rows, width = queries.shape
    row, col = lax.axis_index("row"), lax.axis_index("col")
    experts, inner, feats = w_gate.shape
    steps = feats // width // 2
    hidden = 2 * experts * inner
    tokens = 8 * rows
    sizes = [size for _, size in split_rows(rows)]
    here = jnp.reshape(col, (1,)).astype(jnp.int32)

    ids = jnp.arange(16 * experts, dtype=jnp.int32)
    table = jnp.sum(
        jnp.where(expert_ids[:, :, None] == ids, gate_levels[:, :, None].astype(F32) / 64.0, 0.0), axis=1
    ).astype(BF16)
    paired, siblings, table = attend(
        queries, keys, values, resid, cotangent, doc_ids, row, (w_gate, w_up, w_down), table
    )
    table = jnp.stack(fetch(table, mask_x))
    table = jnp.stack([table, swap(table, mask_y(1))])
    gates = []
    for (start, size), swapped in zip(split_rows(rows), (True, False, True)):
        part = table[:, :, start : start + size]
        gates.append((jnp.swapaxes(part, 0, 1) if swapped else part).reshape(8 * size, -1))
    gates = jnp.concatenate(gates)
    gates = jnp.concatenate(
        [lax.dynamic_slice_in_dim(gates, experts * r, experts, axis=1) for r in (row, row ^ 1)], axis=1
    ).astype(F32)

    paired, gates = tied((paired, gates))
    sib_gate, sib_up, sib_down = siblings
    x = gather_tokens(paired)
    gain = norm_gain.reshape(1, feats)

    cs, xs = part_specs(sizes, width, 0), part_specs(sizes, width, 1)
    ws = weight_spec(w_gate, width)
    gain_spec = pl.BlockSpec((1, 2 * width), lambda f, s: (0, f ^ (s[0] // 2)))
    one = 2 * tokens * hidden * feats
    flat = jax.ShapeDtypeStruct((tokens, hidden), BF16)
    turned = jax.ShapeDtypeStruct((hidden, tokens), BF16)
    kept = pl.BlockSpec(memory_space=pltpu.VMEM)
    gg, gu, act_t, gg_t, gu_t = call(
        hidden_kernel, here, steps,
        cs + xs + [ws] * 6 + [gain_spec, whole((tokens, 4))],
        [kept] * 5, [flat, flat, turned, turned, turned],
        [pltpu.VMEM((tokens, hidden), F32)] * 3 + [pltpu.VMEM((tokens, 128), F32)],
        (*x, *x, w_gate, sib_gate, w_up, sib_up, w_down, sib_down, gain, gates), 3 * one, 8 * tokens * feats,
    )
    outs, shapes = part_specs(sizes, width), part_shapes(sizes, width)

    def piece(i, start):
        at, size = split_rows(rows)[i]
        span = slice(8 * at, 8 * (at + size))
        return call(
            lambda *refs: piece_kernel(PAIR_AXES[i], span, *refs), start, steps,
            [whole((tokens, hidden))] * 2 + [ws] * 4, outs[i], shapes[i], [],
            (gg, gu, w_gate, sib_gate, w_up, sib_up), 2 * one * size // rows, 8 * hidden * feats,
        )

    def weight_grads(which, start, more):
        half = pl.BlockSpec((hidden // 2, tokens), lambda f, s: (which, 0))
        both = pl.BlockSpec((3, experts, inner, 2 * width), lambda f, s: (0, 0, 0, f ^ (s[0] // 2)))
        shape = jax.ShapeDtypeStruct(w_gate.shape, BF16)
        return call(
            lambda *refs: weight_grad_kernel(bool(more), *refs), start, steps,
            [gain_spec] + xs + cs + [half] * 3 + [both] * len(more),
            [ws] * 3 if more else both, [shape] * 3 if more else jax.ShapeDtypeStruct((3, *w_gate.shape), BF16), [],
            (gain, *x, *x, act_t, gg_t, gu_t, *more), 3 * one // 2, 8 * tokens * feats,
        )

    oa, ob, oc = ORDERS
    pa = scatter_first(piece(0, here), oa)
    pb = scatter_first(piece(1, tied((here, pa[0][0, 0, 0, 0, :1]))[0]), ob)
    na = scatter_next(*pa)
    begin, na = tied((here, na))
    begin = tied((begin, pb[0][0, 0, 0, 0, :1]))[0]
    pc = scatter_first(piece(2, begin), oc)
    ra = send_pair(na, oa)
    nb, nc = scatter_next(*pb), scatter_next(*pc)
    begin, ra, nb, nc = tied((here, ra, nb, nc))
    sent = weight_grads(1, begin, ())
    rb, rc = send_pair(nb, ob), send_pair(nc, oc)
    sent, ra, rb, rc = tied((sent, ra, rb, rc))
    parts = [add(*r) for r in (ra, rb, rc)]
    more = swap(sent, mask_core)
    got = [send_three(p, order[1]) for p, order in zip(parts, ORDERS)]
    grads = weight_grads(0, here, (more,))
    got, (d_gate, d_up, d_down) = tied((got, grads))
    got = tied([send_three(add(*g), order[0]) for g, order in zip(got, ORDERS)])
    d_normed = jnp.concatenate([add(*g) for g in got])
    return (d_normed, d_gate, d_up, d_down)


def solution(mesh):
    tile, split3 = P("row", "col"), P("row", "col", None)
    return jax.shard_map(
        body,
        mesh=mesh,
        in_specs=(tile, tile, tile, tile, P(), P(), P("row", None), P("row", None), split3, split3, split3, tile),
        out_specs=(tile, split3, split3, split3),
        check_vma=False,
    )
```

```python
import math

import jax
import jax.numpy as jnp
from jax import lax
from jax.experimental import pallas as pl
from jax.experimental.pallas import tpu as pltpu
from jax.sharding import PartitionSpec as P

HEAD_DIM = 128
WINDOW = 1024
EPS = 1e-05
VMEM = 56 * 2**20
F32, BF16 = jnp.float32, jnp.bfloat16
def mask_core(i):
    return 8


def mask_x(k):
    return lambda i: (k ^ (k & 1) * (i >> 2 & 2)) << 4


def mask_z(k):
    return lambda i: k


def mask_y(k):
    return lambda i: ((k >> 1) << 2) | ((k & 1) << 6)


def swap(x, mask):
    return lax.ppermute(x, ("row", "col"), [(i, i ^ mask(i)) for i in range(128)])


tied = lax.optimization_barrier


def fetch(x, mask):
    return [x, swap(x, mask(1)), swap(x, mask(2)), swap(x, mask(3))]


def add(*terms):
    return sum(t.astype(F32) for t in terms).astype(BF16)


ORDERS = ((mask_z, mask_y, mask_x), (mask_x, mask_z, mask_y), (mask_y, mask_x, mask_z))


def split_rows(rows):
    step = rows // 8
    return ((0, 2 * step), (2 * step, 3 * step), (5 * step, 3 * step))


def gather_tokens(x, beside):
    width = x.shape[1]
    parts = [x[start : start + size] for start, size in split_rows(x.shape[0])]
    for stage in (0, 1):
        got, beside = tied(([fetch(part, order[stage]) for part, order in zip(parts, ORDERS)], beside))
        if stage == 0:
            beside = [beside[0], *(swap(w, mask_core) for w in beside[1:])]
        parts = [jnp.stack(g) for g in got]
    pairs = []
    for i, (part, order) in enumerate(zip(parts, ORDERS)):
        one = swap(part, order[2](1))
        again = tied((part, one))[0] if i == 0 else part
        pairs.append((one, swap(again, order[2](3))))
    pairs = tied(pairs)
    wholes = []
    for part, (one, three), (_, _, last) in zip(parts, pairs, ORDERS):
        wholes.append([part, one, swap(three[:2], last(1)), swap(one[2:], last(3)), three])
    a, b, c = [jnp.concatenate(w) for w in wholes]
    a = a.reshape(4, 2, 2, 4, -1, width)
    b = b.reshape(2, 2, 4, 4, -1, width)
    c = c.reshape(4, 4, 2, 2, -1, width)
    return (a, b, c), beside


def scatter_first(p, order):
    p = p.reshape(4, 4, 4, *p.shape[-2:])
    return p, swap(p[2, :2], order[2](1)), swap(p[2, 2:], order[2](3))


def scatter_next(p, from_one, from_three):
    for_one = jnp.concatenate([p[1, :2], add(p[1, 2:], from_three)])
    for_three = jnp.concatenate([add(p[3, :2], from_one), p[3, 2:]])
    return p[0], for_one, for_three


def send_pair(p, order):
    mine, for_one, for_three = p
    return mine, swap(for_one, order[2](1)), swap(for_three, order[2](3))


def send_three(p, mask):
    return p[0], swap(p[1], mask(1)), swap(p[2], mask(2)), swap(p[3], mask(3))


def part_specs(sizes, width, side=0):
    a, b, c = sizes
    return [
        pl.BlockSpec((4, None, 2, 2, a, width), lambda f, s: (0, f // 2, 0, f % 2, 0, side)),
        pl.BlockSpec((None, 2, 2, 4, b, width), lambda f, s: (f // 2, 0, f % 2, 0, 0, side)),
        pl.BlockSpec((2, 4, None, 2, c, width), lambda f, s: (f % 2, 0, f // 2, 0, 0, side)),
    ]


PAIR_AXES = (2, 1, 0)


def pair_at(axis, i):
    return (slice(None),) * axis + (i,)


def pair_rows(ref, axis, odd):
    sides = [ref[pair_at(axis, i)].reshape(-1, ref.shape[-1]) for i in (odd, 1 - odd)]
    return jnp.concatenate(sides, axis=1)


def stacked(*refs):
    return jnp.concatenate([rows_of(r) for r in refs])


def part_shapes(sizes, width):
    a, b, c = sizes
    return [
        jax.ShapeDtypeStruct((4, 2, 2, 4, a, width), BF16),
        jax.ShapeDtypeStruct((2, 2, 4, 4, b, width), BF16),
        jax.ShapeDtypeStruct((4, 4, 2, 2, c, width), BF16),
    ]


def rows_of(ref):
    return ref[...].reshape(-1, ref.shape[-1])


def dot_nt(a, b):
    return lax.dot_general(a, b, (((1,), (1,)), ((), ())), preferred_element_type=F32)


def dot_nn(a, b):
    return lax.dot_general(a, b, (((1,), (0,)), ((), ())), preferred_element_type=F32)


def weight_spec(w, width):
    return pl.BlockSpec((w.shape[0], w.shape[1], 2 * width), lambda f, s: (0, 0, f ^ (s[0] // 2)))


def whole(shape):
    return pl.BlockSpec(shape, lambda f, s: (0,) * len(shape))


def call(kernel, col, steps, in_specs, out_specs, out_shape, scratch, args, flops, moved):
    return pl.pallas_call(
        kernel,
        out_shape=out_shape,
        grid_spec=pltpu.PrefetchScalarGridSpec(
            num_scalar_prefetch=1,
            grid=(steps,),
            in_specs=in_specs,
            out_specs=out_specs,
            scratch_shapes=scratch,
        ),
        compiler_params=pltpu.CompilerParams(vmem_limit_bytes=VMEM),
        cost_estimate=pl.CostEstimate(flops=flops, bytes_accessed=moved, transcendentals=0),
    )(col, *args)


def attention_kernel(q, own, sib, resid, cot, qdoc, kdoc, qpos, kpos, out):
    width = q.shape[1]
    out[:, :width] = cot[...]
    keys = own.shape[0]
    delta = qpos[...] - kpos[...]
    allowed = (delta >= 0) & (delta < WINDOW) & (qdoc[...] == kdoc[...])
    for h in range(width // HEAD_DIM):
        cols = slice(h * HEAD_DIM, (h + 1) * HEAD_DIM)
        vcols = slice(width + h * HEAD_DIM, width + (h + 1) * HEAD_DIM)
        s = jnp.concatenate([dot_nt(q[:, cols], own[:, cols]), dot_nt(q[:, cols], sib[:, cols])], axis=1)
        s = jnp.where(allowed, s * (1.0 / math.sqrt(HEAD_DIM)), -1e30)
        e = jnp.exp(s - jnp.max(s, axis=1, keepdims=True))
        p = (e / jnp.sum(e, axis=1, keepdims=True)).astype(BF16)
        o = dot_nn(p[:, :keys], own[:, vcols]) + dot_nn(p[:, keys:], sib[:, vcols])
        out[:, vcols] = (resid[:, cols].astype(F32) + o).astype(BF16)


def attend(queries, keys, values, resid, cotangent, doc_ids, row, weights, table):
    rows, width = queries.shape
    reach = WINDOW // rows
    pair = jnp.concatenate([keys, values], axis=1)
    blocks = []
    for by in range(reach, 0, -2):
        blocks.append(lax.ppermute(pair, "row", [(i, i + by) for i in range(16 - by)]))
    blocks, table = tied((blocks, table))
    own = jnp.concatenate(blocks + [pair])
    sib = swap(own, mask_core)
    siblings = [swap(tied((weights[0], sib))[0], mask_core), *weights[1:]]
    padded = jnp.concatenate([jnp.full(((reach + 1) * rows,), -1, jnp.int32), doc_ids])

    def info(r):
        first = r - reach
        docs = lax.dynamic_slice_in_dim(padded, (first + reach + 1) * rows, (reach + 1) * rows)
        pos = first * rows + jnp.arange((reach + 1) * rows, dtype=jnp.int32)
        return docs.reshape(reach + 1, rows)[::2].reshape(1, -1), pos.reshape(reach + 1, rows)[::2].reshape(1, -1)

    (d0, p0), (d1, p1) = info(row), info(row ^ 1)
    kdoc, kpos = jnp.concatenate([d0, d1], axis=1), jnp.concatenate([p0, p1], axis=1)
    kdoc = jnp.where(kpos >= 0, kdoc, -1)
    qdoc = lax.dynamic_slice_in_dim(doc_ids, row * rows, rows)[:, None]
    qpos = row * rows + jnp.arange(rows, dtype=jnp.int32)[:, None]
    out = pl.pallas_call(
        attention_kernel,
        out_shape=jax.ShapeDtypeStruct((rows, 2 * width), BF16),
        compiler_params=pltpu.CompilerParams(vmem_limit_bytes=VMEM),
        cost_estimate=pl.CostEstimate(flops=4 * rows * width * own.shape[0] * 2, bytes_accessed=4 * own.size, transcendentals=0),
    )(queries, own, sib, resid, cotangent, qdoc, kdoc, qpos, kpos)
    return out, siblings, table


def hidden_kernel(
    s, ca, cb, cc, xa, xb, xc, wg0, wg1, wu0, wu1, wd0, wd1, gain, gates,
    gg_out, gu_out, act_t, gg_t, gu_t, g_acc, u_acc, d_acc, sq_acc
):
    f = pl.program_id(0)
    tokens, hidden = g_acc.shape
    odd = s[0] % 2

    def products(first):
        start = 0
        for axis, c, x in zip(PAIR_AXES, (ca, cb, cc), (xa, xb, xc)):
            x = pair_rows(x, axis, odd).astype(F32)
            span = slice(start, start + x.shape[0])
            start += x.shape[0]
            sq = x * x
            total = sq[:, :128]
            for j in range(128, x.shape[1], 128):
                total += sq[:, j : j + 128]
            x = (x * gain[...]).astype(BF16)
            for acc, value in (
                (sq_acc, total),
                (g_acc, dot_nt(x, stacked(wg0, wg1))),
                (u_acc, dot_nt(x, stacked(wu0, wu1))),
                (d_acc, dot_nt(pair_rows(c, axis, odd), stacked(wd0, wd1))),
            ):
                acc[span] = value if first else acc[span] + value

    @pl.when(f == 0)
    def _():
        products(True)

    @pl.when(f > 0)
    def _():
        products(False)

    @pl.when(f == pl.num_programs(0) - 1)
    def _():
        feats = pl.num_programs(0) * 2 * xa.shape[-1]
        expert = lax.broadcasted_iota(jnp.int32, (1, hidden), 1) // (hidden // 4)
        for r in range(0, tokens, 128):
            span = slice(r, r + 128)
            inv = lax.rsqrt(jnp.sum(sq_acc[span], axis=1, keepdims=True) * (1.0 / feats) + EPS)
            gate = jnp.where(
                expert < 2,
                jnp.where(expert == 0, gates[span, 0:1], gates[span, 1:2]),
                jnp.where(expert == 2, gates[span, 2:3], gates[span, 3:4]),
            )
            pre_gate, pre_up = g_acc[span] * inv, u_acc[span] * inv
            sig = jax.nn.sigmoid(pre_gate)
            silu = pre_gate * sig
            grad = d_acc[span] * gate
            gg = grad * pre_up * sig * (1.0 + pre_gate * (1.0 - sig))
            gu = grad * silu
            gg_out[span] = gg.astype(BF16)
            gu_out[span] = gu.astype(BF16)
            act_t[:, span] = (silu * pre_up * gate).T.astype(BF16)
            gg_t[:, span] = (gg * inv).T.astype(BF16)
            gu_t[:, span] = (gu * inv).T.astype(BF16)


def piece_kernel(s, gg, gu, wg0, wg1, wu0, wu1, oa, ob, oc):
    odd = s[0] % 2
    width = oa.shape[-1]
    start = 0
    for axis, o in zip(PAIR_AXES, (oa, ob, oc)):
        size = math.prod(o.shape[:-1]) // 2
        span = slice(start, start + size)
        start += size
        out = dot_nn(gg[span], stacked(wg0, wg1)) + dot_nn(gu[span], stacked(wu0, wu1))
        for i, at in enumerate((odd, 1 - odd)):
            at = pair_at(axis, at)
            o[at] = out[:, i * width : (i + 1) * width].astype(BF16).reshape(o.at[at].shape)


def weight_grad_kernel(with_more, s, gain, *refs):
    xs, cs = refs[:3], refs[3:6]
    act_t, gg_t, gu_t = refs[6:9]
    more = refs[9] if with_more else None
    dg, du, dd = refs[-3:] if with_more else [refs[-1].at[i] for i in range(3)]
    odd = s[0] % 2
    for lhs, data, scale, extra, out in (
        (gg_t, xs, gain, 0, dg),
        (gu_t, xs, gain, 1, du),
        (act_t, cs, None, 2, dd),
    ):
        rows = jnp.concatenate([pair_rows(x, axis, odd) for axis, x in zip(PAIR_AXES, data)])
        total = dot_nn(lhs[...], rows)
        if scale is not None:
            total = total * scale[...]
        if with_more:
            total = total + more[extra].reshape(total.shape).astype(F32)
        out[...] = total.astype(BF16).reshape(out.shape)


def body(
    resid, queries, keys, values, doc_ids, norm_gain, expert_ids, gate_levels, w_gate, w_up, w_down, cotangent
):
    rows, width = queries.shape
    row, col = lax.axis_index("row"), lax.axis_index("col")
    experts, inner, feats = w_gate.shape
    steps = feats // width // 2
    hidden = 2 * experts * inner
    tokens = 8 * rows
    sizes = [size for _, size in split_rows(rows)]
    here = jnp.reshape(col, (1,)).astype(jnp.int32)

    ids = jnp.arange(16 * experts, dtype=jnp.int32)
    table = jnp.sum(
        jnp.where(expert_ids[:, :, None] == ids, gate_levels[:, :, None].astype(F32) / 64.0, 0.0), axis=1
    ).astype(BF16)
    table = jnp.stack(fetch(table, mask_x))
    table = jnp.stack([table, swap(table, mask_y(1))])
    paired, siblings, table = attend(
        queries, keys, values, resid, cotangent, doc_ids, row, (w_gate, w_up, w_down), table
    )
    gates = []
    for (start, size), swapped in zip(split_rows(rows), (True, False, True)):
        part = table[:, :, start : start + size]
        gates.append((jnp.swapaxes(part, 0, 1) if swapped else part).reshape(8 * size, -1))
    gates = jnp.concatenate(gates)
    gates = jnp.concatenate(
        [lax.dynamic_slice_in_dim(gates, experts * r, experts, axis=1) for r in (row, row ^ 1)], axis=1
    ).astype(F32)

    paired, gates = tied((paired, gates))
    x, (sib_gate, sib_up, sib_down) = gather_tokens(paired, siblings)
    gain = norm_gain.reshape(1, feats)

    cs, xs = part_specs(sizes, width, 0), part_specs(sizes, width, 1)
    ws = weight_spec(w_gate, width)
    gain_spec = pl.BlockSpec((1, 2 * width), lambda f, s: (0, f ^ (s[0] // 2)))
    one = 2 * tokens * hidden * feats
    flat = jax.ShapeDtypeStruct((tokens, hidden), BF16)
    turned = jax.ShapeDtypeStruct((hidden, tokens), BF16)
    kept = pl.BlockSpec(memory_space=pltpu.VMEM)
    gg, gu, act_t, gg_t, gu_t = call(
        hidden_kernel, here, steps,
        cs + xs + [ws] * 6 + [gain_spec, whole((tokens, 4))],
        [kept] * 5, [flat, flat, turned, turned, turned],
        [pltpu.VMEM((tokens, hidden), F32)] * 3 + [pltpu.VMEM((tokens, 128), F32)],
        (*x, *x, w_gate, sib_gate, w_up, sib_up, w_down, sib_down, gain, gates), 3 * one, 8 * tokens * feats,
    )
    pieces = call(
        piece_kernel, here, steps, [whole((tokens, hidden))] * 2 + [ws] * 4,
        part_specs(sizes, width), part_shapes(sizes, width), [],
        (gg, gu, w_gate, sib_gate, w_up, sib_up), 2 * one, 4 * tokens * feats,
    )

    def weight_grads(which, start, more):
        half = pl.BlockSpec((hidden // 2, tokens), lambda f, s: (which, 0))
        both = pl.BlockSpec((3, experts, inner, 2 * width), lambda f, s: (0, 0, 0, f ^ (s[0] // 2)))
        shape = jax.ShapeDtypeStruct(w_gate.shape, BF16)
        return call(
            lambda *refs: weight_grad_kernel(bool(more), *refs), start, steps,
            [gain_spec] + xs + cs + [half] * 3 + [both] * len(more),
            [ws] * 3 if more else both, [shape] * 3 if more else jax.ShapeDtypeStruct((3, *w_gate.shape), BF16), [],
            (gain, *x, *x, act_t, gg_t, gu_t, *more), 3 * one // 2, 8 * tokens * feats,
        )

    oa, ob, oc = ORDERS
    pa, pb, pc = pieces
    pa = scatter_first(pa, oa)
    mine, for_one, for_three = scatter_next(*pa)
    begin, for_one, pb, pc = tied((here, for_one, pb, pc))
    pb, pc = scatter_first(pb, ob), scatter_first(pc, oc)
    from_one = swap(for_one, oa[2](1))
    sent = weight_grads(1, begin, ())
    sent, from_one, for_three, pb, pc = tied((sent, from_one, for_three, pb, pc))
    ra = (mine, from_one, swap(for_three, oa[2](3)))
    rb, rc = send_pair(scatter_next(*pb), ob), send_pair(scatter_next(*pc), oc)
    ra, rb, rc = tied((ra, rb, rc))
    parts = [add(*r) for r in (ra, rb, rc)]
    more = swap(sent, mask_core)
    got = [send_three(p, order[1]) for p, order in zip(parts, ORDERS)]
    grads = weight_grads(0, here, (more,))
    got, (d_gate, d_up, d_down) = tied((got, grads))
    got = tied([send_three(add(*g), order[0]) for g, order in zip(got, ORDERS)])
    d_normed = jnp.concatenate([add(*g) for g in got])
    return (d_normed, d_gate, d_up, d_down)


def solution(mesh):
    tile, split3 = P("row", "col"), P("row", "col", None)
    return jax.shard_map(
        body,
        mesh=mesh,
        in_specs=(tile, tile, tile, tile, P(), P(), P("row", None), P("row", None), split3, split3, split3, tile),
        out_specs=(tile, split3, split3, split3),
        check_vma=False,
    )
```

```python
import math

import jax
import jax.numpy as jnp
from jax import lax
from jax.experimental import pallas as pl
from jax.experimental.pallas import tpu as pltpu
from jax.sharding import PartitionSpec as P

HEAD_DIM = 128
WINDOW = 1024
EPS = 1e-05
VMEM = 56 * 2**20
F32, BF16 = jnp.float32, jnp.bfloat16
def mask_core(i):
    return 8


def mask_x(k):
    return lambda i: (k ^ (k & 1) * (i >> 2 & 2)) << 4


def mask_z(k):
    return lambda i: k


def mask_y(k):
    return lambda i: ((k >> 1) << 2) | ((k & 1) << 6)


def swap(x, mask):
    return lax.ppermute(x, ("row", "col"), [(i, i ^ mask(i)) for i in range(128)])


tied = lax.optimization_barrier


def fetch(x, mask):
    return [x, swap(x, mask(1)), swap(x, mask(2)), swap(x, mask(3))]


def add(*terms):
    return sum(t.astype(F32) for t in terms).astype(BF16)


ORDERS = ((mask_z, mask_y, mask_x), (mask_y, mask_x, mask_z))


def split_rows(rows):
    return ((0, rows // 2), (rows // 2, rows // 2))


def gather_tokens(x, beside):
    width = x.shape[1]
    parts = [x[start : start + size] for start, size in split_rows(x.shape[0])]
    for stage in (0, 1):
        got, beside = tied(([fetch(part, order[stage]) for part, order in zip(parts, ORDERS)], beside))
        beside = [swap(w, mask_core) if i == stage + 1 else w for i, w in enumerate(beside)]
        parts = [jnp.stack(g) for g in got]
    pairs = [(swap(part, order[2](1)), swap(part, order[2](3))) for part, order in zip(parts, ORDERS)]
    pairs, beside = tied((pairs, beside))
    a, c = [
        jnp.concatenate([part, one, swap(three[:2], last(1)), swap(one[2:], last(3)), three])
        for part, (one, three), (_, _, last) in zip(parts, pairs, ORDERS)
    ]
    return (a.reshape(4, 2, 2, 4, -1, width), c.reshape(4, 4, 2, 2, -1, width)), beside


def scatter_first(p, order):
    p = p.reshape(4, 4, 4, *p.shape[-2:])
    return p, swap(p[2, :2], order[2](1)), swap(p[2, 2:], order[2](3))


def scatter_next(p, from_one, from_three):
    for_one = jnp.concatenate([p[1, :2], add(p[1, 2:], from_three)])
    for_three = jnp.concatenate([add(p[3, :2], from_one), p[3, 2:]])
    return p[0], for_one, for_three


def send_pair(p, order):
    mine, for_one, for_three = p
    return mine, swap(for_one, order[2](1)), swap(for_three, order[2](3))


def send_three(p, mask):
    return p[0], swap(p[1], mask(1)), swap(p[2], mask(2)), swap(p[3], mask(3))


def part_specs(sizes, width, side=0):
    a, c = sizes
    return [
        pl.BlockSpec((4, None, 2, 2, a, width), lambda f, s: (0, f // 2, 0, f % 2, 0, side)),
        pl.BlockSpec((2, 4, None, 2, c, width), lambda f, s: (f % 2, 0, f // 2, 0, 0, side)),
    ]


PAIR_AXES = (2, 0)


def pair_at(axis, i):
    return (slice(None),) * axis + (i,)


def pair_rows(ref, axis, odd):
    sides = [ref[pair_at(axis, i)].reshape(-1, ref.shape[-1]) for i in (odd, 1 - odd)]
    return jnp.concatenate(sides, axis=1)


def stacked(*refs):
    return jnp.concatenate([rows_of(r) for r in refs])


def part_shapes(sizes, width):
    a, c = sizes
    return [
        jax.ShapeDtypeStruct((4, 2, 2, 4, a, width), BF16),
        jax.ShapeDtypeStruct((4, 4, 2, 2, c, width), BF16),
    ]


def rows_of(ref):
    return ref[...].reshape(-1, ref.shape[-1])


def dot_nt(a, b):
    return lax.dot_general(a, b, (((1,), (1,)), ((), ())), preferred_element_type=F32)


def dot_nn(a, b):
    return lax.dot_general(a, b, (((1,), (0,)), ((), ())), preferred_element_type=F32)


def weight_spec(w, width):
    return pl.BlockSpec((w.shape[0], w.shape[1], 2 * width), lambda f, s: (0, 0, f ^ (s[0] // 2)))


def whole(shape):
    return pl.BlockSpec(shape, lambda f, s: (0,) * len(shape))


def call(kernel, col, steps, in_specs, out_specs, out_shape, scratch, args, flops, moved):
    return pl.pallas_call(
        kernel,
        out_shape=out_shape,
        grid_spec=pltpu.PrefetchScalarGridSpec(
            num_scalar_prefetch=1,
            grid=(steps,),
            in_specs=in_specs,
            out_specs=out_specs,
            scratch_shapes=scratch,
        ),
        compiler_params=pltpu.CompilerParams(vmem_limit_bytes=VMEM),
        cost_estimate=pl.CostEstimate(flops=flops, bytes_accessed=moved, transcendentals=0),
    )(col, *args)


def attention_kernel(q, own, sib, resid, cot, qdoc, kdoc, qpos, kpos, out):
    width = q.shape[1]
    out[:, :width] = cot[...]
    keys = own.shape[0]
    delta = qpos[...] - kpos[...]
    allowed = (delta >= 0) & (delta < WINDOW) & (qdoc[...] == kdoc[...])
    for h in range(width // HEAD_DIM):
        cols = slice(h * HEAD_DIM, (h + 1) * HEAD_DIM)
        vcols = slice(width + h * HEAD_DIM, width + (h + 1) * HEAD_DIM)
        s = jnp.concatenate([dot_nt(q[:, cols], own[:, cols]), dot_nt(q[:, cols], sib[:, cols])], axis=1)
        s = jnp.where(allowed, s * (1.0 / math.sqrt(HEAD_DIM)), -1e30)
        e = jnp.exp(s - jnp.max(s, axis=1, keepdims=True))
        p = (e / jnp.sum(e, axis=1, keepdims=True)).astype(BF16)
        o = dot_nn(p[:, :keys], own[:, vcols]) + dot_nn(p[:, keys:], sib[:, vcols])
        out[:, vcols] = (resid[:, cols].astype(F32) + o).astype(BF16)


def attend(queries, keys, values, resid, cotangent, doc_ids, row, weights, table):
    rows, width = queries.shape
    reach = WINDOW // rows
    pair = jnp.concatenate([keys, values], axis=1)
    blocks = []
    for by in range(reach, 0, -2):
        blocks.append(lax.ppermute(pair, "row", [(i, i + by) for i in range(16 - by)]))
    blocks, table = tied((blocks, table))
    own = jnp.concatenate(blocks + [pair])
    sib = swap(own, mask_core)
    siblings = [swap(tied((weights[0], sib))[0], mask_core), *weights[1:]]
    padded = jnp.concatenate([jnp.full(((reach + 1) * rows,), -1, jnp.int32), doc_ids])

    def info(r):
        first = r - reach
        docs = lax.dynamic_slice_in_dim(padded, (first + reach + 1) * rows, (reach + 1) * rows)
        pos = first * rows + jnp.arange((reach + 1) * rows, dtype=jnp.int32)
        return docs.reshape(reach + 1, rows)[::2].reshape(1, -1), pos.reshape(reach + 1, rows)[::2].reshape(1, -1)

    (d0, p0), (d1, p1) = info(row), info(row ^ 1)
    kdoc, kpos = jnp.concatenate([d0, d1], axis=1), jnp.concatenate([p0, p1], axis=1)
    kdoc = jnp.where(kpos >= 0, kdoc, -1)
    qdoc = lax.dynamic_slice_in_dim(doc_ids, row * rows, rows)[:, None]
    qpos = row * rows + jnp.arange(rows, dtype=jnp.int32)[:, None]
    out = pl.pallas_call(
        attention_kernel,
        out_shape=jax.ShapeDtypeStruct((rows, 2 * width), BF16),
        compiler_params=pltpu.CompilerParams(vmem_limit_bytes=VMEM),
        cost_estimate=pl.CostEstimate(flops=4 * rows * width * own.shape[0] * 2, bytes_accessed=4 * own.size, transcendentals=0),
    )(queries, own, sib, resid, cotangent, qdoc, kdoc, qpos, kpos)
    return out, siblings, table


def hidden_kernel(
    s, ca, cc, xa, xc, wg0, wg1, wu0, wu1, wd0, wd1, gain, gates,
    gg_out, gu_out, act_t, gg_t, gu_t, g_acc, u_acc, d_acc, sq_acc
):
    f = pl.program_id(0)
    tokens, hidden = g_acc.shape
    odd = s[0] % 2

    def products(first):
        start = 0
        for axis, c, x in zip(PAIR_AXES, (ca, cc), (xa, xc)):
            x = pair_rows(x, axis, odd).astype(F32)
            span = slice(start, start + x.shape[0])
            start += x.shape[0]
            sq = x * x
            total = sq[:, :128]
            for j in range(128, x.shape[1], 128):
                total += sq[:, j : j + 128]
            x = (x * gain[...]).astype(BF16)
            for acc, value in (
                (sq_acc, total),
                (g_acc, dot_nt(x, stacked(wg0, wg1))),
                (u_acc, dot_nt(x, stacked(wu0, wu1))),
                (d_acc, dot_nt(pair_rows(c, axis, odd), stacked(wd0, wd1))),
            ):
                acc[span] = value if first else acc[span] + value

    @pl.when(f == 0)
    def _():
        products(True)

    @pl.when(f > 0)
    def _():
        products(False)

    @pl.when(f == pl.num_programs(0) - 1)
    def _():
        feats = pl.num_programs(0) * 2 * xa.shape[-1]
        expert = lax.broadcasted_iota(jnp.int32, (1, hidden), 1) // (hidden // 4)
        for r in range(0, tokens, 128):
            span = slice(r, r + 128)
            inv = lax.rsqrt(jnp.sum(sq_acc[span], axis=1, keepdims=True) * (1.0 / feats) + EPS)
            gate = jnp.where(
                expert < 2,
                jnp.where(expert == 0, gates[span, 0:1], gates[span, 1:2]),
                jnp.where(expert == 2, gates[span, 2:3], gates[span, 3:4]),
            )
            pre_gate, pre_up = g_acc[span] * inv, u_acc[span] * inv
            sig = jax.nn.sigmoid(pre_gate)
            silu = pre_gate * sig
            grad = d_acc[span] * gate
            gg = grad * pre_up * sig * (1.0 + pre_gate * (1.0 - sig))
            gu = grad * silu
            gg_out[span] = gg.astype(BF16)
            gu_out[span] = gu.astype(BF16)
            act_t[:, span] = (silu * pre_up * gate).T.astype(BF16)
            gg_t[:, span] = (gg * inv).T.astype(BF16)
            gu_t[:, span] = (gu * inv).T.astype(BF16)


def piece_kernel(s, gg, gu, wg0, wg1, wu0, wu1, oa, oc):
    odd = s[0] % 2
    width = oa.shape[-1]
    start = 0
    for axis, o in zip(PAIR_AXES, (oa, oc)):
        size = math.prod(o.shape[:-1]) // 2
        span = slice(start, start + size)
        start += size
        out = dot_nn(gg[span], stacked(wg0, wg1)) + dot_nn(gu[span], stacked(wu0, wu1))
        for i, at in enumerate((odd, 1 - odd)):
            at = pair_at(axis, at)
            o[at] = out[:, i * width : (i + 1) * width].astype(BF16).reshape(o.at[at].shape)


def weight_grad_kernel(with_more, s, gain, *refs):
    xs, cs = refs[:2], refs[2:4]
    act_t, gg_t, gu_t = refs[4:7]
    more = refs[7] if with_more else None
    dg, du, dd = refs[-3:] if with_more else [refs[-1].at[i] for i in range(3)]
    odd = s[0] % 2
    for lhs, data, scale, extra, out in (
        (gg_t, xs, gain, 0, dg),
        (gu_t, xs, gain, 1, du),
        (act_t, cs, None, 2, dd),
    ):
        rows = jnp.concatenate([pair_rows(x, axis, odd) for axis, x in zip(PAIR_AXES, data)])
        total = dot_nn(lhs[...], rows)
        if scale is not None:
            total = total * scale[...]
        if with_more:
            total = total + more[extra].reshape(total.shape).astype(F32)
        out[...] = total.astype(BF16).reshape(out.shape)


def body(
    resid, queries, keys, values, doc_ids, norm_gain, expert_ids, gate_levels, w_gate, w_up, w_down, cotangent
):
    rows, width = queries.shape
    row, col = lax.axis_index("row"), lax.axis_index("col")
    experts, inner, feats = w_gate.shape
    steps = feats // width // 2
    hidden = 2 * experts * inner
    tokens = 8 * rows
    sizes = [size for _, size in split_rows(rows)]
    here = jnp.reshape(col, (1,)).astype(jnp.int32)

    ids = jnp.arange(16 * experts, dtype=jnp.int32)
    table = jnp.sum(
        jnp.where(expert_ids[:, :, None] == ids, gate_levels[:, :, None].astype(F32) / 64.0, 0.0), axis=1
    ).astype(BF16)
    table = jnp.stack(fetch(table, mask_x))
    table = jnp.stack([table, swap(table, mask_y(1))])
    paired, siblings, table = attend(
        queries, keys, values, resid, cotangent, doc_ids, row, (w_gate, w_up, w_down), table
    )
    gates = []
    for start, size in split_rows(rows):
        gates.append(jnp.swapaxes(table[:, :, start : start + size], 0, 1).reshape(8 * size, -1))
    gates = jnp.concatenate(gates)
    gates = jnp.concatenate(
        [lax.dynamic_slice_in_dim(gates, experts * r, experts, axis=1) for r in (row, row ^ 1)], axis=1
    ).astype(F32)

    paired, gates = tied((paired, gates))
    x, (sib_gate, sib_up, sib_down) = gather_tokens(paired, siblings)
    gain = norm_gain.reshape(1, feats)

    cs, xs = part_specs(sizes, width, 0), part_specs(sizes, width, 1)
    ws = weight_spec(w_gate, width)
    gain_spec = pl.BlockSpec((1, 2 * width), lambda f, s: (0, f ^ (s[0] // 2)))
    one = 2 * tokens * hidden * feats
    flat = jax.ShapeDtypeStruct((tokens, hidden), BF16)
    turned = jax.ShapeDtypeStruct((hidden, tokens), BF16)
    kept = pl.BlockSpec(memory_space=pltpu.VMEM)
    gg, gu, act_t, gg_t, gu_t = call(
        hidden_kernel, here, steps,
        cs + xs + [ws] * 6 + [gain_spec, whole((tokens, 4))],
        [kept] * 5, [flat, flat, turned, turned, turned],
        [pltpu.VMEM((tokens, hidden), F32)] * 3 + [pltpu.VMEM((tokens, 128), F32)],
        (*x, *x, w_gate, sib_gate, w_up, sib_up, w_down, sib_down, gain, gates), 3 * one, 8 * tokens * feats,
    )
    pieces = call(
        piece_kernel, here, steps, [whole((tokens, hidden))] * 2 + [ws] * 4,
        part_specs(sizes, width), part_shapes(sizes, width), [],
        (gg, gu, w_gate, sib_gate, w_up, sib_up), 2 * one, 4 * tokens * feats,
    )

    def weight_grads(which, start, more):
        half = pl.BlockSpec((hidden // 2, tokens), lambda f, s: (which, 0))
        both = pl.BlockSpec((3, experts, inner, 2 * width), lambda f, s: (0, 0, 0, f ^ (s[0] // 2)))
        shape = jax.ShapeDtypeStruct(w_gate.shape, BF16)
        return call(
            lambda *refs: weight_grad_kernel(bool(more), *refs), start, steps,
            [gain_spec] + xs + cs + [half] * 3 + [both] * len(more),
            [ws] * 3 if more else both, [shape] * 3 if more else jax.ShapeDtypeStruct((3, *w_gate.shape), BF16), [],
            (gain, *x, *x, act_t, gg_t, gu_t, *more), 3 * one // 2, 8 * tokens * feats,
        )

    pieces = [scatter_first(p, order) for p, order in zip(pieces, ORDERS)]
    sent, pieces = tied((weight_grads(1, here, ()), pieces))
    got = [send_pair(scatter_next(*p), order) for p, order in zip(pieces, ORDERS)]
    got, (d_gate, d_up, d_down) = tied((got, weight_grads(0, here, (swap(sent, mask_core),))))
    for stage in (1, 0):
        got = tied([send_three(add(*g), order[stage]) for g, order in zip(got, ORDERS)])
    d_normed = jnp.concatenate([add(*g) for g in got])
    return (d_normed, d_gate, d_up, d_down)


def solution(mesh):
    tile, split3 = P("row", "col"), P("row", "col", None)
    return jax.shard_map(
        body,
        mesh=mesh,
        in_specs=(tile, tile, tile, tile, P(), P(), P("row", None), P("row", None), split3, split3, split3, tile),
        out_specs=(tile, split3, split3, split3),
        check_vma=False,
    )
```

```python
import math

import jax
import jax.numpy as jnp
from jax import lax
from jax.experimental import pallas as pl
from jax.experimental.pallas import tpu as pltpu
from jax.sharding import PartitionSpec as P

HEAD_DIM = 128
WINDOW = 1024
EPS = 1e-05
VMEM = 56 * 2**20
F32, BF16 = jnp.float32, jnp.bfloat16
def mask_core(i):
    return 8


def mask_x(k):
    return lambda i: (k ^ (k & 1) * (i >> 2 & 2)) << 4


def mask_z(k):
    return lambda i: k


def mask_y(k):
    return lambda i: ((k >> 1) << 2) | ((k & 1) << 6)


def swap(x, mask):
    return lax.ppermute(x, ("row", "col"), [(i, i ^ mask(i)) for i in range(128)])


tied = lax.optimization_barrier


def fetch(x, mask):
    return [x, swap(x, mask(1)), swap(x, mask(2)), swap(x, mask(3))]


def add(*terms):
    return sum(t.astype(F32) for t in terms).astype(BF16)


ORDERS = ((mask_z, mask_y, mask_x), (mask_y, mask_x, mask_z))


def split_rows(rows):
    return ((0, rows // 2), (rows // 2, rows // 2))


def neighbours(parts, stage):
    return [(swap(part, order[stage](1)), swap(part, order[stage](3))) for part, order in zip(parts, ORDERS)]


def far_side(parts, pairs, stage):
    got = []
    for part, (one, three), order in zip(parts, pairs, ORDERS):
        got.append([part, one, swap(three[:2], order[stage](1)), swap(one[2:], order[stage](3)), three])
    return got


def gather_tokens(x, weights, table):
    width = x.shape[1]
    first, second, third = weights
    parts = [x[start : start + size] for start, size in split_rows(x.shape[0])]
    got, first, second = tied(([fetch(part, order[0]) for part, order in zip(parts, ORDERS)], first, second))
    parts = [jnp.stack(g) for g in got]
    second = swap(second, mask_core)
    pairs, second = tied((neighbours(parts, 1), second))
    got, table, third = tied((far_side(parts, pairs, 1), table, third))
    parts = [jnp.concatenate(g).reshape(4, 4, -1, width) for g in got]
    table = jnp.stack(fetch(table, mask_x))
    table = jnp.stack([table, swap(table, mask_y(1))])
    pairs, table, third = tied((neighbours(parts, 2), table, third))
    third = swap(third, mask_core)
    a, c = [jnp.concatenate(g) for g in far_side(parts, pairs, 2)]
    return (a.reshape(4, 2, 2, 4, -1, width), c.reshape(4, 4, 2, 2, -1, width)), (first, second, third), table


def scatter_first(p, order):
    p = p.reshape(4, 4, 4, *p.shape[-2:])
    return p, swap(p[2, :2], order[2](1)), swap(p[2, 2:], order[2](3))


def scatter_next(p, from_one, from_three):
    for_one = jnp.concatenate([p[1, :2], add(p[1, 2:], from_three)])
    for_three = jnp.concatenate([add(p[3, :2], from_one), p[3, 2:]])
    return p[0], for_one, for_three


def send_pair(p, order):
    mine, for_one, for_three = p
    return mine, swap(for_one, order[2](1)), swap(for_three, order[2](3))


def send_three(p, mask):
    return p[0], swap(p[1], mask(1)), swap(p[2], mask(2)), swap(p[3], mask(3))


def part_specs(sizes, width, side=0):
    a, c = sizes
    return [
        pl.BlockSpec((4, None, 2, 2, a, width), lambda f, s: (0, f // 2, 0, f % 2, 0, side)),
        pl.BlockSpec((2, 4, None, 2, c, width), lambda f, s: (f % 2, 0, f // 2, 0, 0, side)),
    ]


PAIR_AXES = (2, 0)


def pair_at(axis, i):
    return (slice(None),) * axis + (i,)


def pair_rows(ref, axis, odd):
    sides = [ref[pair_at(axis, i)].reshape(-1, ref.shape[-1]) for i in (odd, 1 - odd)]
    return jnp.concatenate(sides, axis=1)


def stacked(*refs):
    return jnp.concatenate([rows_of(r) for r in refs])


def part_shapes(sizes, width):
    a, c = sizes
    return [
        jax.ShapeDtypeStruct((4, 2, 2, 4, a, width), BF16),
        jax.ShapeDtypeStruct((4, 4, 2, 2, c, width), BF16),
    ]


def rows_of(ref):
    return ref[...].reshape(-1, ref.shape[-1])


def dot_nt(a, b):
    return lax.dot_general(a, b, (((1,), (1,)), ((), ())), preferred_element_type=F32)


def dot_nn(a, b):
    return lax.dot_general(a, b, (((1,), (0,)), ((), ())), preferred_element_type=F32)


def weight_spec(w, width):
    return pl.BlockSpec((w.shape[0], w.shape[1], 2 * width), lambda f, s: (0, 0, f ^ (s[0] // 2)))


def whole(shape):
    return pl.BlockSpec(shape, lambda f, s: (0,) * len(shape))


def call(kernel, col, steps, in_specs, out_specs, out_shape, scratch, args, flops, moved):
    return pl.pallas_call(
        kernel,
        out_shape=out_shape,
        grid_spec=pltpu.PrefetchScalarGridSpec(
            num_scalar_prefetch=1,
            grid=(steps,),
            in_specs=in_specs,
            out_specs=out_specs,
            scratch_shapes=scratch,
        ),
        compiler_params=pltpu.CompilerParams(vmem_limit_bytes=VMEM),
        cost_estimate=pl.CostEstimate(flops=flops, bytes_accessed=moved, transcendentals=0),
    )(col, *args)


def attention_kernel(q, own, sib, resid, cot, qdoc, kdoc, qpos, kpos, out):
    width = q.shape[1]
    out[:, :width] = cot[...]
    keys = own.shape[0]
    delta = qpos[...] - kpos[...]
    allowed = (delta >= 0) & (delta < WINDOW) & (qdoc[...] == kdoc[...])
    for h in range(width // HEAD_DIM):
        cols = slice(h * HEAD_DIM, (h + 1) * HEAD_DIM)
        vcols = slice(width + h * HEAD_DIM, width + (h + 1) * HEAD_DIM)
        s = jnp.concatenate([dot_nt(q[:, cols], own[:, cols]), dot_nt(q[:, cols], sib[:, cols])], axis=1)
        s = jnp.where(allowed, s * (1.0 / math.sqrt(HEAD_DIM)), -1e30)
        e = jnp.exp(s - jnp.max(s, axis=1, keepdims=True))
        p = (e / jnp.sum(e, axis=1, keepdims=True)).astype(BF16)
        o = dot_nn(p[:, :keys], own[:, vcols]) + dot_nn(p[:, keys:], sib[:, vcols])
        out[:, vcols] = (resid[:, cols].astype(F32) + o).astype(BF16)


def attend(queries, keys, values, resid, cotangent, doc_ids, row, weights):
    rows, width = queries.shape
    reach = WINDOW // rows
    pair = jnp.concatenate([keys, values], axis=1)
    blocks = []
    for by in range(reach, 0, -2):
        blocks.append(lax.ppermute(pair, "row", [(i, i + by) for i in range(16 - by)]))
    own = jnp.concatenate(blocks + [pair])
    sib = swap(own, mask_core)
    siblings = [swap(tied((weights[0], sib))[0], mask_core), *weights[1:]]
    padded = jnp.concatenate([jnp.full(((reach + 1) * rows,), -1, jnp.int32), doc_ids])

    def info(r):
        first = r - reach
        docs = lax.dynamic_slice_in_dim(padded, (first + reach + 1) * rows, (reach + 1) * rows)
        pos = first * rows + jnp.arange((reach + 1) * rows, dtype=jnp.int32)
        return docs.reshape(reach + 1, rows)[::2].reshape(1, -1), pos.reshape(reach + 1, rows)[::2].reshape(1, -1)

    (d0, p0), (d1, p1) = info(row), info(row ^ 1)
    kdoc, kpos = jnp.concatenate([d0, d1], axis=1), jnp.concatenate([p0, p1], axis=1)
    kdoc = jnp.where(kpos >= 0, kdoc, -1)
    qdoc = lax.dynamic_slice_in_dim(doc_ids, row * rows, rows)[:, None]
    qpos = row * rows + jnp.arange(rows, dtype=jnp.int32)[:, None]
    out = pl.pallas_call(
        attention_kernel,
        out_shape=jax.ShapeDtypeStruct((rows, 2 * width), BF16),
        compiler_params=pltpu.CompilerParams(vmem_limit_bytes=VMEM),
        cost_estimate=pl.CostEstimate(flops=4 * rows * width * own.shape[0] * 2, bytes_accessed=4 * own.size, transcendentals=0),
    )(queries, own, sib, resid, cotangent, qdoc, kdoc, qpos, kpos)
    return out, siblings


def hidden_kernel(
    s, ca, cc, xa, xc, wg0, wg1, wu0, wu1, wd0, wd1, gain, gates,
    gg_out, gu_out, act_t, gg_t, gu_t, g_acc, u_acc, d_acc, sq_acc
):
    f = pl.program_id(0)
    tokens, hidden = g_acc.shape
    odd = s[0] % 2

    def products(first):
        start = 0
        for axis, c, x in zip(PAIR_AXES, (ca, cc), (xa, xc)):
            x = pair_rows(x, axis, odd).astype(F32)
            span = slice(start, start + x.shape[0])
            start += x.shape[0]
            sq = x * x
            total = sq[:, :128]
            for j in range(128, x.shape[1], 128):
                total += sq[:, j : j + 128]
            x = (x * gain[...]).astype(BF16)
            for acc, value in (
                (sq_acc, total),
                (g_acc, dot_nt(x, stacked(wg0, wg1))),
                (u_acc, dot_nt(x, stacked(wu0, wu1))),
                (d_acc, dot_nt(pair_rows(c, axis, odd), stacked(wd0, wd1))),
            ):
                acc[span] = value if first else acc[span] + value

    @pl.when(f == 0)
    def _():
        products(True)

    @pl.when(f > 0)
    def _():
        products(False)

    @pl.when(f == pl.num_programs(0) - 1)
    def _():
        feats = pl.num_programs(0) * 2 * xa.shape[-1]
        expert = lax.broadcasted_iota(jnp.int32, (1, hidden), 1) // (hidden // 4)
        for r in range(0, tokens, 128):
            span = slice(r, r + 128)
            inv = lax.rsqrt(jnp.sum(sq_acc[span], axis=1, keepdims=True) * (1.0 / feats) + EPS)
            gate = jnp.where(
                expert < 2,
                jnp.where(expert == 0, gates[span, 0:1], gates[span, 1:2]),
                jnp.where(expert == 2, gates[span, 2:3], gates[span, 3:4]),
            )
            pre_gate, pre_up = g_acc[span] * inv, u_acc[span] * inv
            sig = jax.nn.sigmoid(pre_gate)
            silu = pre_gate * sig
            grad = d_acc[span] * gate
            gg = grad * pre_up * sig * (1.0 + pre_gate * (1.0 - sig))
            gu = grad * silu
            gg_out[span] = gg.astype(BF16)
            gu_out[span] = gu.astype(BF16)
            act_t[:, span] = (silu * pre_up * gate).T.astype(BF16)
            gg_t[:, span] = (gg * inv).T.astype(BF16)
            gu_t[:, span] = (gu * inv).T.astype(BF16)


def piece_kernel(s, gg, gu, wg0, wg1, wu0, wu1, oa, oc):
    odd = s[0] % 2
    width = oa.shape[-1]
    start = 0
    for axis, o in zip(PAIR_AXES, (oa, oc)):
        size = math.prod(o.shape[:-1]) // 2
        span = slice(start, start + size)
        start += size
        out = dot_nn(gg[span], stacked(wg0, wg1)) + dot_nn(gu[span], stacked(wu0, wu1))
        for i, at in enumerate((odd, 1 - odd)):
            at = pair_at(axis, at)
            o[at] = out[:, i * width : (i + 1) * width].astype(BF16).reshape(o.at[at].shape)


def weight_grad_kernel(with_more, s, gain, *refs):
    xs, cs = refs[:2], refs[2:4]
    act_t, gg_t, gu_t = refs[4:7]
    more = refs[7] if with_more else None
    dg, du, dd = refs[-3:] if with_more else [refs[-1].at[i] for i in range(3)]
    odd = s[0] % 2
    for lhs, data, scale, extra, out in (
        (gg_t, xs, gain, 0, dg),
        (gu_t, xs, gain, 1, du),
        (act_t, cs, None, 2, dd),
    ):
        rows = jnp.concatenate([pair_rows(x, axis, odd) for axis, x in zip(PAIR_AXES, data)])
        total = dot_nn(lhs[...], rows)
        if scale is not None:
            total = total * scale[...]
        if with_more:
            total = total + more[extra].reshape(total.shape).astype(F32)
        out[...] = total.astype(BF16).reshape(out.shape)


def body(
    resid, queries, keys, values, doc_ids, norm_gain, expert_ids, gate_levels, w_gate, w_up, w_down, cotangent
):
    rows, width = queries.shape
    row, col = lax.axis_index("row"), lax.axis_index("col")
    experts, inner, feats = w_gate.shape
    steps = feats // width // 2
    hidden = 2 * experts * inner
    tokens = 8 * rows
    sizes = [size for _, size in split_rows(rows)]
    here = jnp.reshape(col, (1,)).astype(jnp.int32)

    ids = jnp.arange(16 * experts, dtype=jnp.int32)
    table = jnp.sum(
        jnp.where(expert_ids[:, :, None] == ids, gate_levels[:, :, None].astype(F32) / 64.0, 0.0), axis=1
    ).astype(BF16)
    paired, siblings = attend(queries, keys, values, resid, cotangent, doc_ids, row, (w_gate, w_up, w_down))
    x, (sib_gate, sib_up, sib_down), table = gather_tokens(paired, siblings, table)
    gates = []
    for start, size in split_rows(rows):
        gates.append(jnp.swapaxes(table[:, :, start : start + size], 0, 1).reshape(8 * size, -1))
    gates = jnp.concatenate(gates)
    gates = jnp.concatenate(
        [lax.dynamic_slice_in_dim(gates, experts * r, experts, axis=1) for r in (row, row ^ 1)], axis=1
    ).astype(F32)

    gain = norm_gain.reshape(1, feats)

    cs, xs = part_specs(sizes, width, 0), part_specs(sizes, width, 1)
    ws = weight_spec(w_gate, width)
    gain_spec = pl.BlockSpec((1, 2 * width), lambda f, s: (0, f ^ (s[0] // 2)))
    one = 2 * tokens * hidden * feats
    flat = jax.ShapeDtypeStruct((tokens, hidden), BF16)
    turned = jax.ShapeDtypeStruct((hidden, tokens), BF16)
    kept = pl.BlockSpec(memory_space=pltpu.VMEM)
    gg, gu, act_t, gg_t, gu_t = call(
        hidden_kernel, here, steps,
        cs + xs + [ws] * 6 + [gain_spec, whole((tokens, 4))],
        [kept] * 5, [flat, flat, turned, turned, turned],
        [pltpu.VMEM((tokens, hidden), F32)] * 3 + [pltpu.VMEM((tokens, 128), F32)],
        (*x, *x, w_gate, sib_gate, w_up, sib_up, w_down, sib_down, gain, gates), 3 * one, 8 * tokens * feats,
    )
    pieces = call(
        piece_kernel, here, steps, [whole((tokens, hidden))] * 2 + [ws] * 4,
        part_specs(sizes, width), part_shapes(sizes, width), [],
        (gg, gu, w_gate, sib_gate, w_up, sib_up), 2 * one, 4 * tokens * feats,
    )

    def weight_grads(which, start, more):
        half = pl.BlockSpec((hidden // 2, tokens), lambda f, s: (which, 0))
        both = pl.BlockSpec((3, experts, inner, 2 * width), lambda f, s: (0, 0, 0, f ^ (s[0] // 2)))
        shape = jax.ShapeDtypeStruct(w_gate.shape, BF16)
        return call(
            lambda *refs: weight_grad_kernel(bool(more), *refs), start, steps,
            [gain_spec] + xs + cs + [half] * 3 + [both] * len(more),
            [ws] * 3 if more else both, [shape] * 3 if more else jax.ShapeDtypeStruct((3, *w_gate.shape), BF16), [],
            (gain, *x, *x, act_t, gg_t, gu_t, *more), 3 * one // 2, 8 * tokens * feats,
        )

    pieces = [scatter_first(p, order) for p, order in zip(pieces, ORDERS)]
    sent, pieces = tied((weight_grads(1, here, ()), pieces))
    got = [send_pair(scatter_next(*p), order) for p, order in zip(pieces, ORDERS)]
    got, (d_gate, d_up, d_down) = tied((got, weight_grads(0, here, (swap(sent, mask_core),))))
    for stage in (1, 0):
        got = tied([send_three(add(*g), order[stage]) for g, order in zip(got, ORDERS)])
    d_normed = jnp.concatenate([add(*g) for g in got])
    return (d_normed, d_gate, d_up, d_down)


def solution(mesh):
    tile, split3 = P("row", "col"), P("row", "col", None)
    return jax.shard_map(
        body,
        mesh=mesh,
        in_specs=(tile, tile, tile, tile, P(), P(), P("row", None), P("row", None), split3, split3, split3, tile),
        out_specs=(tile, split3, split3, split3),
        check_vma=False,
    )
```

```python
import math

import jax
import jax.numpy as jnp
from jax import lax
from jax.experimental import pallas as pl
from jax.experimental.pallas import tpu as pltpu
from jax.sharding import PartitionSpec as P

HEAD_DIM = 128
WINDOW = 1024
EPS = 1e-05
VMEM = 56 * 2**20
F32, BF16 = jnp.float32, jnp.bfloat16
def mask_core(i):
    return 8


def mask_x(k):
    return lambda i: (k ^ (k & 1) * (i >> 2 & 2)) << 4


def mask_z(k):
    return lambda i: k


def mask_y(k):
    return lambda i: ((k >> 1) << 2) | ((k & 1) << 6)


def swap(x, mask):
    return lax.ppermute(x, ("row", "col"), [(i, i ^ mask(i)) for i in range(128)])


tied = lax.optimization_barrier


def fetch(x, mask):
    return [x, swap(x, mask(1)), swap(x, mask(2)), swap(x, mask(3))]


def add(*terms):
    return sum(t.astype(F32) for t in terms).astype(BF16)


ORDERS = ((mask_z, mask_y, mask_x), (mask_y, mask_x, mask_z))


def split_rows(rows):
    return ((0, rows // 2), (rows // 2, rows // 2))


def neighbours(parts, stage):
    return [(swap(part, order[stage](1)), swap(part, order[stage](3))) for part, order in zip(parts, ORDERS)]


def far_side(parts, pairs, stage):
    got = []
    for part, (one, three), order in zip(parts, pairs, ORDERS):
        got.append([part, one, swap(three[:2], order[stage](1)), swap(one[2:], order[stage](3)), three])
    return got


def gather_tokens(x, weights, table):
    width = x.shape[1]
    first, second, third = weights
    parts = [x[start : start + size] for start, size in split_rows(x.shape[0])]
    got = [fetch(part, order[0]) for part, order in zip(parts, ORDERS)]
    got, first, second, table = tied((got, first, second, table))
    parts = [jnp.stack(g) for g in got]
    second = swap(second, mask_core)
    pairs, second, table = tied((neighbours(parts, 1), second, jnp.stack(table)))
    got, third, *table = tied((far_side(parts, pairs, 1), third, table, swap(table, mask_y(1))))
    parts = [jnp.concatenate(g).reshape(4, 4, -1, width) for g in got]
    third = swap(third, mask_core)
    pairs, third = tied((neighbours(parts, 2), third))
    a, c = [jnp.concatenate(g) for g in far_side(parts, pairs, 2)]
    return (a.reshape(4, 2, 2, 4, -1, width), c.reshape(4, 4, 2, 2, -1, width)), (first, second, third), jnp.stack(table)


def scatter_first(p, order):
    p = p.reshape(4, 4, 4, *p.shape[-2:])
    return p, swap(p[2, :2], order[2](1)), swap(p[2, 2:], order[2](3))


def scatter_next(p, from_one, from_three):
    for_one = jnp.concatenate([p[1, :2], add(p[1, 2:], from_three)])
    for_three = jnp.concatenate([add(p[3, :2], from_one), p[3, 2:]])
    return p[0], for_one, for_three


def send_pair(p, order):
    mine, for_one, for_three = p
    return mine, swap(for_one, order[2](1)), swap(for_three, order[2](3))


def send_three(p, mask):
    return p[0], swap(p[1], mask(1)), swap(p[2], mask(2)), swap(p[3], mask(3))


def part_specs(sizes, width, side=0):
    a, c = sizes
    return [
        pl.BlockSpec((4, None, 2, 2, a, width), lambda f, s: (0, f // 2, 0, f % 2, 0, side)),
        pl.BlockSpec((2, 4, None, 2, c, width), lambda f, s: (f % 2, 0, f // 2, 0, 0, side)),
    ]


PAIR_AXES = (2, 0)


def pair_at(axis, i):
    return (slice(None),) * axis + (i,)


def pair_rows(ref, axis, odd):
    sides = [ref[pair_at(axis, i)].reshape(-1, ref.shape[-1]) for i in (odd, 1 - odd)]
    return jnp.concatenate(sides, axis=1)


def stacked(*refs):
    return jnp.concatenate([rows_of(r) for r in refs])


def part_shapes(sizes, width):
    a, c = sizes
    return [
        jax.ShapeDtypeStruct((4, 2, 2, 4, a, width), BF16),
        jax.ShapeDtypeStruct((4, 4, 2, 2, c, width), BF16),
    ]


def rows_of(ref):
    return ref[...].reshape(-1, ref.shape[-1])


def dot_nt(a, b):
    return lax.dot_general(a, b, (((1,), (1,)), ((), ())), preferred_element_type=F32)


def dot_nn(a, b):
    return lax.dot_general(a, b, (((1,), (0,)), ((), ())), preferred_element_type=F32)


def weight_spec(w, width):
    return pl.BlockSpec((w.shape[0], w.shape[1], 2 * width), lambda f, s: (0, 0, f ^ (s[0] // 2)))


def whole(shape):
    return pl.BlockSpec(shape, lambda f, s: (0,) * len(shape))


def call(kernel, col, steps, in_specs, out_specs, out_shape, scratch, args, flops, moved):
    return pl.pallas_call(
        kernel,
        out_shape=out_shape,
        grid_spec=pltpu.PrefetchScalarGridSpec(
            num_scalar_prefetch=1,
            grid=(steps,),
            in_specs=in_specs,
            out_specs=out_specs,
            scratch_shapes=scratch,
        ),
        compiler_params=pltpu.CompilerParams(vmem_limit_bytes=VMEM),
        cost_estimate=pl.CostEstimate(flops=flops, bytes_accessed=moved, transcendentals=0),
    )(col, *args)


def attention_kernel(q, own, sib, resid, cot, qdoc, kdoc, qpos, kpos, out):
    width = q.shape[1]
    out[:, :width] = cot[...]
    keys = own.shape[0]
    delta = qpos[...] - kpos[...]
    allowed = (delta >= 0) & (delta < WINDOW) & (qdoc[...] == kdoc[...])
    for h in range(width // HEAD_DIM):
        cols = slice(h * HEAD_DIM, (h + 1) * HEAD_DIM)
        vcols = slice(width + h * HEAD_DIM, width + (h + 1) * HEAD_DIM)
        s = jnp.concatenate([dot_nt(q[:, cols], own[:, cols]), dot_nt(q[:, cols], sib[:, cols])], axis=1)
        s = jnp.where(allowed, s * (1.0 / math.sqrt(HEAD_DIM)), -1e30)
        e = jnp.exp(s - jnp.max(s, axis=1, keepdims=True))
        p = (e / jnp.sum(e, axis=1, keepdims=True)).astype(BF16)
        o = dot_nn(p[:, :keys], own[:, vcols]) + dot_nn(p[:, keys:], sib[:, vcols])
        out[:, vcols] = (resid[:, cols].astype(F32) + o).astype(BF16)


def attend(queries, keys, values, resid, cotangent, doc_ids, row, weights, table):
    rows, width = queries.shape
    reach = WINDOW // rows
    pair = jnp.concatenate([keys, values], axis=1)
    blocks = []
    for by in range(reach, 0, -2):
        blocks.append(lax.ppermute(pair, "row", [(i, i + by) for i in range(16 - by)]))
    blocks, table = tied((blocks, table))
    table = fetch(table, mask_x)
    own = jnp.concatenate(blocks + [pair])
    sib = swap(own, mask_core)
    siblings = [swap(tied((weights[0], sib))[0], mask_core), *weights[1:]]
    padded = jnp.concatenate([jnp.full(((reach + 1) * rows,), -1, jnp.int32), doc_ids])

    def info(r):
        first = r - reach
        docs = lax.dynamic_slice_in_dim(padded, (first + reach + 1) * rows, (reach + 1) * rows)
        pos = first * rows + jnp.arange((reach + 1) * rows, dtype=jnp.int32)
        return docs.reshape(reach + 1, rows)[::2].reshape(1, -1), pos.reshape(reach + 1, rows)[::2].reshape(1, -1)

    (d0, p0), (d1, p1) = info(row), info(row ^ 1)
    kdoc, kpos = jnp.concatenate([d0, d1], axis=1), jnp.concatenate([p0, p1], axis=1)
    kdoc = jnp.where(kpos >= 0, kdoc, -1)
    qdoc = lax.dynamic_slice_in_dim(doc_ids, row * rows, rows)[:, None]
    qpos = row * rows + jnp.arange(rows, dtype=jnp.int32)[:, None]
    out = pl.pallas_call(
        attention_kernel,
        out_shape=jax.ShapeDtypeStruct((rows, 2 * width), BF16),
        compiler_params=pltpu.CompilerParams(vmem_limit_bytes=VMEM),
        cost_estimate=pl.CostEstimate(flops=4 * rows * width * own.shape[0] * 2, bytes_accessed=4 * own.size, transcendentals=0),
    )(queries, own, sib, resid, cotangent, qdoc, kdoc, qpos, kpos)
    return out, siblings, table


def hidden_kernel(
    s, ca, cc, xa, xc, wg0, wg1, wu0, wu1, wd0, wd1, gain, gates,
    gg_out, gu_out, act_t, gg_t, gu_t, g_acc, u_acc, d_acc, sq_acc
):
    f = pl.program_id(0)
    tokens, hidden = g_acc.shape
    odd = s[0] % 2

    def products(first):
        start = 0
        for axis, c, x in zip(PAIR_AXES, (ca, cc), (xa, xc)):
            x = pair_rows(x, axis, odd).astype(F32)
            span = slice(start, start + x.shape[0])
            start += x.shape[0]
            sq = x * x
            total = sq[:, :128]
            for j in range(128, x.shape[1], 128):
                total += sq[:, j : j + 128]
            x = (x * gain[...]).astype(BF16)
            for acc, value in (
                (sq_acc, total),
                (g_acc, dot_nt(x, stacked(wg0, wg1))),
                (u_acc, dot_nt(x, stacked(wu0, wu1))),
                (d_acc, dot_nt(pair_rows(c, axis, odd), stacked(wd0, wd1))),
            ):
                acc[span] = value if first else acc[span] + value

    @pl.when(f == 0)
    def _():
        products(True)

    @pl.when(f > 0)
    def _():
        products(False)

    @pl.when(f == pl.num_programs(0) - 1)
    def _():
        feats = pl.num_programs(0) * 2 * xa.shape[-1]
        expert = lax.broadcasted_iota(jnp.int32, (1, hidden), 1) // (hidden // 4)
        for r in range(0, tokens, 128):
            span = slice(r, r + 128)
            inv = lax.rsqrt(jnp.sum(sq_acc[span], axis=1, keepdims=True) * (1.0 / feats) + EPS)
            gate = jnp.where(
                expert < 2,
                jnp.where(expert == 0, gates[span, 0:1], gates[span, 1:2]),
                jnp.where(expert == 2, gates[span, 2:3], gates[span, 3:4]),
            )
            pre_gate, pre_up = g_acc[span] * inv, u_acc[span] * inv
            sig = jax.nn.sigmoid(pre_gate)
            silu = pre_gate * sig
            grad = d_acc[span] * gate
            gg = grad * pre_up * sig * (1.0 + pre_gate * (1.0 - sig))
            gu = grad * silu
            gg_out[span] = gg.astype(BF16)
            gu_out[span] = gu.astype(BF16)
            act_t[:, span] = (silu * pre_up * gate).T.astype(BF16)
            gg_t[:, span] = (gg * inv).T.astype(BF16)
            gu_t[:, span] = (gu * inv).T.astype(BF16)


def piece_kernel(s, gg, gu, wg0, wg1, wu0, wu1, oa, oc):
    odd = s[0] % 2
    width = oa.shape[-1]
    start = 0
    for axis, o in zip(PAIR_AXES, (oa, oc)):
        size = math.prod(o.shape[:-1]) // 2
        span = slice(start, start + size)
        start += size
        out = dot_nn(gg[span], stacked(wg0, wg1)) + dot_nn(gu[span], stacked(wu0, wu1))
        for i, at in enumerate((odd, 1 - odd)):
            at = pair_at(axis, at)
            o[at] = out[:, i * width : (i + 1) * width].astype(BF16).reshape(o.at[at].shape)


def weight_grad_kernel(with_more, s, gain, *refs):
    xs, cs = refs[:2], refs[2:4]
    act_t, gg_t, gu_t = refs[4:7]
    more = refs[7] if with_more else None
    dg, du, dd = refs[-3:] if with_more else [refs[-1].at[i] for i in range(3)]
    odd = s[0] % 2
    for lhs, data, scale, extra, out in (
        (gg_t, xs, gain, 0, dg),
        (gu_t, xs, gain, 1, du),
        (act_t, cs, None, 2, dd),
    ):
        rows = jnp.concatenate([pair_rows(x, axis, odd) for axis, x in zip(PAIR_AXES, data)])
        total = dot_nn(lhs[...], rows)
        if scale is not None:
            total = total * scale[...]
        if with_more:
            total = total + more[extra].reshape(total.shape).astype(F32)
        out[...] = total.astype(BF16).reshape(out.shape)


def body(
    resid, queries, keys, values, doc_ids, norm_gain, expert_ids, gate_levels, w_gate, w_up, w_down, cotangent
):
    rows, width = queries.shape
    row, col = lax.axis_index("row"), lax.axis_index("col")
    experts, inner, feats = w_gate.shape
    steps = feats // width // 2
    hidden = 2 * experts * inner
    tokens = 8 * rows
    sizes = [size for _, size in split_rows(rows)]
    here = jnp.reshape(col, (1,)).astype(jnp.int32)

    ids = jnp.arange(16 * experts, dtype=jnp.int32)
    table = jnp.sum(
        jnp.where(expert_ids[:, :, None] == ids, gate_levels[:, :, None].astype(F32) / 64.0, 0.0), axis=1
    ).astype(BF16)
    paired, siblings, table = attend(
        queries, keys, values, resid, cotangent, doc_ids, row, (w_gate, w_up, w_down), table
    )
    x, (sib_gate, sib_up, sib_down), table = gather_tokens(paired, siblings, table)
    gates = []
    for start, size in split_rows(rows):
        gates.append(jnp.swapaxes(table[:, :, start : start + size], 0, 1).reshape(8 * size, -1))
    gates = jnp.concatenate(gates)
    gates = jnp.concatenate(
        [lax.dynamic_slice_in_dim(gates, experts * r, experts, axis=1) for r in (row, row ^ 1)], axis=1
    ).astype(F32)

    gain = norm_gain.reshape(1, feats)

    cs, xs = part_specs(sizes, width, 0), part_specs(sizes, width, 1)
    ws = weight_spec(w_gate, width)
    gain_spec = pl.BlockSpec((1, 2 * width), lambda f, s: (0, f ^ (s[0] // 2)))
    one = 2 * tokens * hidden * feats
    flat = jax.ShapeDtypeStruct((tokens, hidden), BF16)
    turned = jax.ShapeDtypeStruct((hidden, tokens), BF16)
    kept = pl.BlockSpec(memory_space=pltpu.VMEM)
    gg, gu, act_t, gg_t, gu_t = call(
        hidden_kernel, here, steps,
        cs + xs + [ws] * 6 + [gain_spec, whole((tokens, 4))],
        [kept] * 5, [flat, flat, turned, turned, turned],
        [pltpu.VMEM((tokens, hidden), F32)] * 3 + [pltpu.VMEM((tokens, 128), F32)],
        (*x, *x, w_gate, sib_gate, w_up, sib_up, w_down, sib_down, gain, gates), 3 * one, 8 * tokens * feats,
    )
    pieces = call(
        piece_kernel, here, steps, [whole((tokens, hidden))] * 2 + [ws] * 4,
        part_specs(sizes, width), part_shapes(sizes, width), [],
        (gg, gu, w_gate, sib_gate, w_up, sib_up), 2 * one, 4 * tokens * feats,
    )

    def weight_grads(which, start, more):
        half = pl.BlockSpec((hidden // 2, tokens), lambda f, s: (which, 0))
        both = pl.BlockSpec((3, experts, inner, 2 * width), lambda f, s: (0, 0, 0, f ^ (s[0] // 2)))
        shape = jax.ShapeDtypeStruct(w_gate.shape, BF16)
        return call(
            lambda *refs: weight_grad_kernel(bool(more), *refs), start, steps,
            [gain_spec] + xs + cs + [half] * 3 + [both] * len(more),
            [ws] * 3 if more else both, [shape] * 3 if more else jax.ShapeDtypeStruct((3, *w_gate.shape), BF16), [],
            (gain, *x, *x, act_t, gg_t, gu_t, *more), 3 * one // 2, 8 * tokens * feats,
        )

    pieces = [scatter_first(p, order) for p, order in zip(pieces, ORDERS)]
    sent, pieces = tied((weight_grads(1, here, ()), pieces))
    got = [send_pair(scatter_next(*p), order) for p, order in zip(pieces, ORDERS)]
    got, (d_gate, d_up, d_down) = tied((got, weight_grads(0, here, (swap(sent, mask_core),))))
    for stage in (1, 0):
        got = tied([send_three(add(*g), order[stage]) for g, order in zip(got, ORDERS)])
    d_normed = jnp.concatenate([add(*g) for g in got])
    return (d_normed, d_gate, d_up, d_down)


def solution(mesh):
    tile, split3 = P("row", "col"), P("row", "col", None)
    return jax.shard_map(
        body,
        mesh=mesh,
        in_specs=(tile, tile, tile, tile, P(), P(), P("row", None), P("row", None), split3, split3, split3, tile),
        out_specs=(tile, split3, split3, split3),
        check_vma=False,
    )
```
